512 devices in a mesh: turn: 32 (over y, x, core), river: 16 (over z).
Axes of the slice: x: 4, y: 4, z: 16, core: 2. Of those that a mesh axis runs over, the one named last changes fastest.
Arguments:
- opener_reach: float32 [4, 1326], replicated, may hold values from 0.0001 to 0.0015
- responder_reach: float32 [4, 1326], replicated, may hold values from 0.0001 to 0.0015
- turn_parent: int32 [96], replicated, may hold values from 0 to 3
- turn_cards: int32 [32], P('turn'), may hold values from 0 to 51
- river_cards: int32 [32, 32], P('turn', 'river'), may hold values from 0 to 51
- showdown_ranks: int32 [32, 32, 1326], P('turn', 'river'), may hold values from 0 to 7461
- fold_mask: int32 [96, 2], replicated, may hold values 0 or 1
- half_pot: float32 [96, 2], replicated, may hold values from 1 to 8
- turn_regrets: float32 [32, 96, 1326], P('turn', 'river'), may hold values from 0.001 to 0.3
- river_regrets: float32 [32, 32, 96, 2, 1326], P('turn', 'river'), may hold values from 0.001 to 0.3
Outputs:
- new_turn_regrets: float32 [32, 96, 1326], P('turn', 'river')
- new_river_regrets: float32 [32, 32, 96, 2, 1326], P('turn', 'river')
- flop_values: float32 [2, 4, 1326], replicated
The draws below stay inside these ranges and needn't reach their ends.
Inputs may be any that keep to these rules, and one draw needn't show every extreme that they name: `showdown_ranks`: higher ranks win, equal ranks tie.
All inputs are finite; a program needn't handle non-finite values.
Results may differ from the reference program's by a relative error of at most 0.0003.
Values sent between devices are 32-bit elements; how exact they have to be, the bound alone decides.
A program may use at most 64 MiB of HBM per device.

```python
import math
import jax
import jax.numpy as jnp
import numpy as np
from jax import lax

H = 1326
FLOP_LINES = 4
RIVER_ACTIONS = 2
RANK_LEVELS = 7462
TURNS = 32
RIVERS = 32
TURN_LINES = 96


def place_ends(drawn, key, low, largest):
    place = [jax.random.randint(jax.random.fold_in(key, axis), (), 0, length) for axis, length in enumerate(drawn.shape)]
    widest = drawn.shape.index(max(drawn.shape))
    next_to = place[:widest] + [(place[widest] + 1) % drawn.shape[widest]] + place[widest + 1:]
    return drawn.at[tuple(place)].set(low).at[tuple(next_to)].set(largest)


def levels(key, shape, cuts, low, largest):
    def one(axis_at, parts):
        steps = jax.random.uniform(jax.random.fold_in(jax.random.fold_in(key, 6), axis_at), (parts,), jnp.float32, low / len(cuts), largest / len(cuts))
        return jnp.repeat(jnp.exp(steps), shape[axis_at] // parts).reshape((-1,) + (1,) * (len(shape) - axis_at - 1))

    loudness = one(*cuts[0])
    for cut in cuts[1:]:
        loudness = loudness * one(*cut)
    return loudness


def setup_inputs(seed: int = 0) -> dict:
    key_of = jax.random.split(jax.random.key(seed), 11)
    opener_reach = jnp.clip(jax.random.uniform(key_of[0], (FLOP_LINES, H), jnp.float32, 0.0001, 0.0015), 0.0001, 0.0015)
    responder_reach = jnp.clip(jax.random.uniform(key_of[1], (FLOP_LINES, H), jnp.float32, 0.0001, 0.0015), 0.0001, 0.0015)
    turn_parent = place_ends(jax.random.randint(key_of[2], (TURN_LINES,), 0, FLOP_LINES), jax.random.fold_in(key_of[2], 1), 0, FLOP_LINES - 1).astype(jnp.int32)
    turn_cards = place_ends(jax.random.randint(key_of[3], (TURNS,), 0, 52), jax.random.fold_in(key_of[3], 1), 0, 51).astype(jnp.int32)
    river_cards = place_ends(jax.random.randint(key_of[4], (TURNS, RIVERS), 0, 52), jax.random.fold_in(key_of[4], 1), 0, 51).astype(jnp.int32)
    showdown_ranks = place_ends(jax.random.randint(key_of[5], (TURNS, RIVERS, H), 0, RANK_LEVELS), jax.random.fold_in(key_of[5], 1), 0, RANK_LEVELS - 1).astype(jnp.int32)
    fold_mask = place_ends((jax.random.randint(key_of[6], (TURN_LINES, RIVER_ACTIONS), 0, 3) < 1).astype(jnp.int32), jax.random.fold_in(key_of[6], 1), 0, 1)
    half_pot = jnp.clip(jnp.exp(jax.random.uniform(key_of[7], (TURN_LINES, RIVER_ACTIONS), jnp.float32, math.log(1.0), math.log(8.0))), 1.0, 8.0)
    turn_regrets = jnp.clip(jnp.exp(math.log(0.3) - 5.7037825 * jax.random.uniform(key_of[8], (TURNS, TURN_LINES, H), jnp.float32) ** levels(key_of[8], (TURNS, TURN_LINES, H), ((0, 32), (1, 16)), -0.2, 0.2)), 0.001, 0.3)
    river_regrets = jnp.clip(jnp.exp(math.log(0.3) - 5.7037825 * jax.random.uniform(key_of[9], (TURNS, RIVERS, TURN_LINES, RIVER_ACTIONS, H), jnp.float32) ** levels(key_of[9], (TURNS, RIVERS, TURN_LINES, RIVER_ACTIONS, H), ((0, 32), (1, 16)), -0.2, 0.2)), 0.001, 0.3)
    return {"opener_reach": opener_reach, "responder_reach": responder_reach, "turn_parent": turn_parent, "turn_cards": turn_cards, "river_cards": river_cards, "showdown_ranks": showdown_ranks, "fold_mask": fold_mask, "half_pot": half_pot, "turn_regrets": turn_regrets, "river_regrets": river_regrets}


HIGH = lax.Precision.HIGHEST


def hand_cards(hand_count):
    low_index, high_index = np.triu_indices(52, 1)
    return jnp.asarray(low_index[:hand_count], dtype=jnp.int32), jnp.asarray(high_index[:hand_count], dtype=jnp.int32)


def card_table(low_card, high_card):
    deck_cards = jnp.arange(52, dtype=jnp.int32)
    holding = (low_card[:, None] == deck_cards[None, :]) | (high_card[:, None] == deck_cards[None, :])
    return holding.astype(jnp.float32)


def unblocked(card_hits, ranges):
    per_card = jnp.dot(ranges, card_hits, precision=HIGH)
    return jnp.sum(ranges, axis=-1, keepdims=True) - jnp.dot(per_card, card_hits.T, precision=HIGH) + ranges


def living_hands(low_card, high_card, turn_card, river_card):
    dead = (low_card == turn_card) | (high_card == turn_card) | (low_card == river_card) | (high_card == river_card)
    return 1.0 - dead.astype(jnp.float32)


def sign_matrix(board_ranks, low_card, high_card):
    shared = (low_card[:, None] == low_card[None, :]) | (low_card[:, None] == high_card[None, :]) | (high_card[:, None] == low_card[None, :]) | (high_card[:, None] == high_card[None, :])
    signs = jnp.sign(board_ranks[None, :] - board_ranks[:, None]).astype(jnp.float32)
    return jnp.where(shared, 0.0, signs).astype(jnp.bfloat16)


def river_finish(living, responder_eff, opener_eff, shown_responder, shown_opener, strategy, regrets_board, fold_mask, half_pot, card_hits):
    hand_count = living.shape[0]
    folded = fold_mask.astype(jnp.float32)[:, :, None]
    stakes = half_pot[:, :, None] * living[None, None, :]
    opener_free = unblocked(card_hits, responder_eff)[:, None, :]
    responder_free = unblocked(card_hits, opener_eff.reshape(-1, hand_count)).reshape(opener_eff.shape)
    opener_value = stakes * ((1.0 - folded) * shown_responder[:, None, :] - folded * opener_free)
    responder_value = stakes * ((1.0 - folded) * shown_opener + folded * responder_free)
    opener_node = jnp.sum(strategy * opener_value, axis=1)
    new_regrets = jnp.maximum(regrets_board + opener_value - opener_node[:, None, :], 0.0)
    responder_node = jnp.sum(responder_value, axis=1)
    return new_regrets, opener_node, responder_node


def reference(opener_reach, responder_reach, turn_parent, turn_cards, river_cards, showdown_ranks, fold_mask, half_pot, turn_regrets, river_regrets):
    low_card, high_card = hand_cards(H)
    card_hits = card_table(low_card, high_card)
    parent_hot = (turn_parent[:, None] == jnp.arange(FLOP_LINES, dtype=jnp.int32)[None, :]).astype(jnp.float32)
    opener_lines = jnp.dot(parent_hot, opener_reach, precision=HIGH)
    responder_base = jnp.dot(parent_hot, responder_reach, precision=HIGH)

    def per_turn(items):
        turn_card, cards_turn, ranks_turn, turn_reg, river_reg = items
        sibling = jnp.dot(parent_hot, jnp.dot(parent_hot.T, turn_reg, precision=HIGH), precision=HIGH)
        turn_strategy = turn_reg / sibling
        responder_lines = responder_base * turn_strategy

        def per_river(inner):
            river_card, board_ranks, regrets_board = inner
            living = living_hands(low_card, high_card, turn_card, river_card)
            strategy = regrets_board / jnp.sum(regrets_board, axis=1, keepdims=True)
            responder_eff = living[None, :] * responder_lines
            opener_eff = living[None, None, :] * opener_lines[:, None, :] * strategy
            matrix = sign_matrix(board_ranks, low_card, high_card)
            shown_responder = jnp.dot(responder_eff.astype(jnp.bfloat16), matrix, preferred_element_type=jnp.float32)
            shown_opener = jnp.dot(opener_eff.reshape(-1, H).astype(jnp.bfloat16), matrix, preferred_element_type=jnp.float32).reshape(opener_eff.shape)
            return river_finish(living, responder_eff, opener_eff, shown_responder, shown_opener, strategy, regrets_board, fold_mask, half_pot, card_hits)

        new_river, opener_nodes, responder_nodes = lax.map(per_river, (cards_turn, ranks_turn, river_reg))
        line_opener = jnp.sum(opener_nodes, axis=0) / RIVERS
        line_responder = jnp.sum(responder_nodes, axis=0) / RIVERS
        node_opener = jnp.dot(parent_hot.T, line_opener, precision=HIGH)
        node_responder = jnp.dot(parent_hot.T, turn_strategy * line_responder, precision=HIGH)
        new_turn = jnp.maximum(turn_reg + line_responder - jnp.dot(parent_hot, node_responder, precision=HIGH), 0.0)
        return new_turn, new_river, node_opener, node_responder

    new_turn, new_river, node_opener, node_responder = lax.map(per_turn, (turn_cards, river_cards, showdown_ranks, turn_regrets, river_regrets))
    flop_values = jnp.stack([jnp.sum(node_opener, axis=0) / TURNS, jnp.sum(node_responder, axis=0) / TURNS])
    return new_turn, new_river, flop_values
```

```python
import jax
import jax.numpy as jnp
import numpy as np
from jax import lax
from jax.experimental import pallas as pl
from jax.experimental.pallas import tpu as pltpu
from jax.sharding import PartitionSpec as P

MESH = pl.DeviceIdType.MESH
F32 = jnp.float32
BF16 = jnp.bfloat16

H = 1326
HP = 1408
L = 96
F = 4
Z = 16
OWN = L // Z
BOARDS = 2
HALF = 768
STEP = 16
STAGES = Z // 4
MIB = 2**20
GROUPS = (slice(0, 512), slice(512, 1024), slice(1024, H))


def tables():
    low, high = np.triu_indices(52, 1)
    holds = np.zeros((HP, 64), np.float32)
    holds[np.arange(H), low] = 1.0
    holds[np.arange(H), high] = 1.0
    clear = (holds @ holds.T == 0).astype(np.float32)
    clear[H:] = 0.0
    clear[:, H:] = 0.0
    counts = holds.copy()
    counts[:H, 52] = 1.0
    spread = -holds.T.copy()
    spread[52, :H] = 1.0
    spreads = np.concatenate([spread, spread, spread, np.zeros_like(spread)], 0)
    cards = np.full((8, HP), -1, np.int32)
    cards[0, :H] = low
    cards[1, :H] = high
    return (
        clear.astype(BF16),
        np.tile(counts, (2, 2)).astype(BF16),
        spreads.astype(BF16),
        cards,
    )


def split(value):
    high = value.astype(BF16)
    return high, (value - high.astype(F32)).astype(BF16)


def dot(a, b):
    return jnp.dot(a, b, preferred_element_type=F32)


def column(row):
    return jnp.broadcast_to(row, (128, row.shape[1])).T


def wide(tile, lanes):
    width = lanes.stop - lanes.start
    return jnp.concatenate([tile] * (-(-width // 128)), 1)[:, :width]


def rows_of(step, start=0):
    return pl.ds(pl.multiple_of(step * STEP + start, STEP), STEP)


def kernel(
    opener_hbm,
    responder_hbm,
    parent_hbm,
    turn_card_hbm,
    river_cards_hbm,
    ranks_hbm,
    fold_hbm,
    pot_hbm,
    counts_hbm,
    spreads_hbm,
    cards_hbm,
    clear_hbm,
    own_hbm,
    river_hbm,
    new_turn,
    new_river,
    flop,
    opener_reach,
    responder_reach,
    parent_row,
    turn_card,
    river_cards,
    ranks,
    fold,
    pot,
    counts,
    spreads,
    cards,
    clear,
    regrets,
    gathered,
    turn_lines,
    signs,
    inverse,
    opener_lines,
    strategy,
    responder_lines,
    high,
    low,
    shown,
    free,
    columns,
    living,
    rank_rows,
    rank_columns,
    opener_total,
    responder_total,
    lines,
    parts,
    part_slots,
    part_sum,
    all_nodes,
    plane_slots,
    plane_sum,
    row_slots,
    final,
    finals,
    next_slots,
    sum_slots,
    sum_out,
    small_sems,
    clear_sem,
    own_sem,
    in_sems,
    turn_sem,
    line_sems,
    out_sems,
    gather_send,
    gather_recv,
    next_send,
    next_recv,
    sum_send,
    sum_recv,
    part_send,
    part_recv,
    node_send,
    node_recv,
    plane_send,
    plane_recv,
    row_send,
    row_recv,
    final_send,
    final_recv,
):
    me = lax.axis_index("river")
    turn = lax.axis_index("turn")
    row, place = turn // 8, lax.rem(turn, 8)

    def along(distance):
        return (turn, lax.rem(me + distance + Z, Z))

    line_peers = [along(d) for d in range(1, Z)]
    plane_peers = [(row * 8 + lax.rem(place + d, 8), me) for d in range(1, 8)]
    row_peers = [(lax.rem(row + d, 4) * 8 + place, me) for d in range(1, 4)]
    everyone = line_peers + plane_peers + row_peers
    barrier = pltpu.get_barrier_semaphore()
    for peer in everyone:
        pl.semaphore_signal(barrier, inc=1, device_id=peer, device_id_type=MESH)

    def block_of(ref, owner):
        return ref.at[pl.ds(lax.rem(owner + Z, Z) * OWN, OWN)]

    def remote(src, dst, send, recv, peer):
        return pltpu.make_async_remote_copy(
            src_ref=src,
            dst_ref=dst,
            send_sem=send,
            recv_sem=recv,
            device_id=peer,
            device_id_type=MESH,
        )

    def start(copies):
        for copy in copies:
            copy.start()

    def arrive(copies):
        for copy in copies:
            copy.wait_recv()

    own_load = pltpu.make_async_copy(own_hbm, block_of(gathered, me), own_sem)
    own_load.start()
    smalls = [
        pltpu.make_async_copy(src, dst, small_sems.at[i])
        for i, (src, dst) in enumerate(
            (
                (opener_hbm, opener_reach),
                (responder_hbm, responder_reach),
                (parent_hbm, parent_row),
                (turn_card_hbm, turn_card),
                (river_cards_hbm, river_cards),
                (ranks_hbm, ranks),
                (fold_hbm, fold),
                (pot_hbm, pot),
                (cards_hbm, cards),
                (counts_hbm, counts),
                (spreads_hbm, spreads),
            )
        )
    ]
    start(smalls)
    loads = [
        [
            pltpu.make_async_copy(
                river_hbm.at[0, b, :, k, :], regrets.at[b, k], in_sems.at[b, k]
            )
            for k in range(2)
        ]
        for b in range(BOARDS)
    ]
    clear_load = pltpu.make_async_copy(clear_hbm, clear, clear_sem)
    start(loads[0])
    clear_load.start()
    start(loads[1])
    for copy in smalls:
        copy.wait()

    gathers = [
        [
            [
                remote(
                    block_of(gathered, me - sign * 2 * stage),
                    block_of(gathered, me - sign * 2 * stage),
                    gather_send.at[way, stage, far],
                    gather_recv.at[way, stage, far],
                    along(sign * (1 + far)),
                )
                for far in range(1 if sign < 0 and stage == STAGES - 1 else 2)
            ]
            for stage in range(STAGES)
        ]
        for way, sign in enumerate((1, -1))
    ]

    def gather_stage(stage):
        for way in gathers:
            if stage:
                way[stage - 1][1].wait_recv()
            start(way[stage])

    def gather_end():
        for way in gathers:
            for stage in range(STAGES):
                way[stage][0].wait_recv()
        gathers[0][-1][1].wait_recv()

    own_load.wait()
    pl.semaphore_wait(barrier, len(everyone))
    gather_stage(0)

    parents = parent_row[...].astype(F32)
    columns[0] = column(parents)
    for k in range(2):
        folded = fold[k : k + 1, :].astype(F32)
        stake = pot[k : k + 1, :]
        columns[1 + k] = column(stake * (1.0 - folded))
        columns[3 + k] = column(stake * folded)
    for b in range(BOARDS):
        dead = jnp.zeros((1, HP), jnp.bool_)
        for card in (turn_card[...], river_cards[:, b : b + 1]):
            dead = dead | (cards[0:1, :] == card) | (cards[1:2, :] == card)
        living[b] = jnp.broadcast_to(jnp.where(dead, 0.0, 1.0).astype(F32), (STEP, HP))
    rank_rows[:, HP - 128 :] = jnp.zeros((8, 128), F32)
    rank_rows[0:BOARDS, 0:H] = ranks[0].astype(F32)
    high[:, HP - 128 :] = jnp.zeros((3 * L, 128), BF16)
    low[:, HP - 128 :] = jnp.zeros((3 * L, 128), BF16)
    responder_total[:, HP - 128 :] = jnp.zeros((L, 128), F32)
    for b in range(BOARDS):
        for c in range(HP // 128):
            tile = slice(c * 128, c * 128 + 128)
            rank_columns[b, tile, :] = column(rank_rows[b : b + 1, tile])

    def of_parent(reach, rows, lanes):
        parent = wide(columns[0, rows, :], lanes)
        line = jnp.broadcast_to(reach[0:1, lanes], parent.shape)
        for f in range(1, F):
            line = jnp.where(parent == f, reach[f : f + 1, lanes], line)
        return line

    @pl.loop(0, L // STEP, unroll=True)
    def _(step):
        rows = rows_of(step)
        for lanes in GROUPS:
            opener_lines[rows, lanes] = of_parent(opener_reach, rows, lanes)

    def free_of(start, size):
        part = slice(start, start + size)
        per_card = dot(jnp.concatenate([high[part, :], low[part, :]], 1), counts[...])
        first = per_card.astype(BF16)
        rest = per_card - first.astype(F32)
        second = rest.astype(BF16)
        third = (rest - second.astype(F32)).astype(BF16)
        lane = lax.broadcasted_iota(jnp.int32, (size, 128), 1)
        left = jnp.where(lane < 64, first.astype(F32), second.astype(F32)).astype(BF16)
        free[part, :] = dot(jnp.concatenate([left, third], 1), spreads[...])

    def sign_rows(b, rows):
        for lanes in (*GROUPS[:2], slice(1024, HP)):
            gap = rank_rows[b : b + 1, lanes] - wide(rank_columns[b, rows, :], lanes)
            sign = jnp.clip(gap, -1.0, 1.0).astype(BF16)
            signs[b, rows, lanes] = sign * clear[rows, lanes]

    def show(b, begin, size, signing=None):
        part = slice(begin, begin + size)
        chunks = range(0, HP, 256)
        steps = HP // STEP
        for i, at in enumerate(chunks):
            out = slice(at, min(at + 256, HP))
            shown[part, out] = dot(high[part, :], signs[b, :, out])
            if signing is not None:

                @pl.loop(i * steps // len(chunks), (i + 1) * steps // len(chunks), unroll=True)
                def _(step):
                    sign_rows(signing, rows_of(step))

    def opener_ranges(b):
        for copy in loads[b]:
            copy.wait()

        @pl.loop(0, L // STEP, unroll=True)
        def _(step):
            rows = rows_of(step)
            for lanes in GROUPS:
                r0, r1 = regrets[b, 0, rows, lanes], regrets[b, 1, rows, lanes]
                inv = 1.0 / (r0 + r1)
                inverse[b, rows, lanes] = inv
                base = opener_lines[rows, lanes] * living[b, :, lanes] * inv
                for k, r in enumerate((r0, r1)):
                    top, rest = split(base * r)
                    high[rows_of(step, k * L), lanes] = top
                    low[rows_of(step, k * L), lanes] = rest

    def line_copy(step):
        rows = rows_of(step)
        return pltpu.make_async_copy(
            responder_total.at[rows], lines.at[rows, 0, :], line_sems.at[step]
        )

    def responder_values(b):
        @pl.loop(0, L // STEP, unroll=True)
        def _(step):
            rows = rows_of(step)
            for lanes in GROUPS:
                base = opener_lines[rows, lanes] * living[b, :, lanes] * inverse[b, rows, lanes]
                value = jnp.zeros(base.shape, F32)
                for k in range(2):
                    line = rows_of(step, k * L)
                    clean = free[line, lanes] + base * regrets[b, k, rows, lanes]
                    value = value + wide(columns[1 + k, rows, :], lanes) * shown[line, lanes]
                    value = value + wide(columns[3 + k, rows, :], lanes) * clean
                value = value * living[b, :, lanes]
                if b == 0:
                    responder_total[rows, lanes] = value
                else:
                    responder_total[rows, lanes] += value
            if b == 1:
                line_copy(step).start()

    clear_load.wait()

    @pl.loop(0, HP // STEP, unroll=True)
    def _(step):
        sign_rows(0, rows_of(step))

    gather_stage(1)
    opener_ranges(0)
    show(0, 0, 2 * L, signing=1)
    gather_stage(2)
    free_of(0, 2 * L)
    responder_values(0)
    opener_ranges(1)
    gather_stage(3)
    show(1, 0, 2 * L)
    free_of(0, 2 * L)
    responder_values(1)

    nexts = [
        [
            remote(
                block_of(lines, me + sign * (7 - 2 * stage)),
                next_slots.at[way, stage],
                next_send.at[way, stage],
                next_recv.at[way, stage],
                along(sign),
            )
            for stage in range(STAGES)
        ]
        for way, sign in enumerate((1, -1))
    ]
    sums = [
        [
            remote(
                sum_out.at[way, stage - 1] if stage else block_of(lines, me + 8),
                sum_slots.at[way, stage],
                sum_send.at[way, stage],
                sum_recv.at[way, stage],
                along(2 * sign),
            )
            if stage or sign > 0
            else None
            for stage in range(STAGES)
        ]
        for way, sign in enumerate((1, -1))
    ]

    def reduce_stage(stage):
        for way, sign in enumerate((1, -1)):
            if stage:
                total = block_of(lines, me + sign * (8 - 2 * stage))[...]
                nexts[way][stage - 1].wait_recv()
                total = total + next_slots[way, stage - 1]
                if stage > 1 or sign > 0:
                    sums[way][stage - 1].wait_recv()
                    total = total + sum_slots[way, stage - 1]
                sum_out[way, stage - 1] = total
            if stage or sign > 0:
                sums[way][stage].start()
            nexts[way][stage].start()

    @pl.loop(0, L // STEP, unroll=True)
    def _(step):
        line_copy(step).wait()

    reduce_stage(0)
    gather_end()
    turn_load = pltpu.make_async_copy(gathered.at[:, 0, :], turn_lines, turn_sem)
    turn_load.start()

    turn_load.wait()

    @pl.loop(0, L // STEP, unroll=True)
    def _(step):
        rows = rows_of(step)
        for lanes in GROUPS:
            top, rest = split(turn_lines[rows, lanes])
            high[rows, lanes] = top
            low[rows, lanes] = rest

    same = (columns[0, :, 0:L] == parents).astype(F32).astype(BF16)
    shown[0:L, :] = dot(same, high[0:L, :]) + dot(same, low[0:L, :])

    @pl.loop(0, L // STEP, unroll=True)
    def _(step):
        rows = rows_of(step)
        for lanes in GROUPS:
            share = turn_lines[rows, lanes] / shown[rows, lanes]
            strategy[rows, lanes] = share
            responder_lines[rows, lanes] = of_parent(responder_reach, rows, lanes) * share

    stores = []
    for b in range(BOARDS):

        @pl.loop(0, L // STEP, unroll=True)
        def _(step):
            rows = rows_of(step)
            for lanes in GROUPS:
                top, rest = split(responder_lines[rows, lanes] * living[b, :, lanes])
                high[rows_of(step, 2 * L), lanes] = top
                low[rows_of(step, 2 * L), lanes] = rest

        show(b, 2 * L, L)
        free_of(2 * L, L)
        if b == 0:
            reduce_stage(1)

        @pl.loop(0, L // STEP, unroll=True)
        def _(step):
            rows = rows_of(step)
            line = rows_of(step, 2 * L)
            for lanes in GROUPS:
                live = living[b, :, lanes]
                inv = inverse[b, rows, lanes]
                won = shown[line, lanes] * live
                lost = (free[line, lanes] + responder_lines[rows, lanes]) * live
                old, values = [], []
                node = jnp.zeros(live.shape, F32)
                for k in range(2):
                    old.append(regrets[b, k, rows, lanes])
                    values.append(
                        wide(columns[1 + k, rows, :], lanes) * won
                        - wide(columns[3 + k, rows, :], lanes) * lost
                    )
                    node = node + old[k] * inv * values[k]
                for k in range(2):
                    regrets[b, k, rows, lanes] = jnp.maximum(old[k] + values[k] - node, 0.0)
                if b == 0:
                    opener_total[rows, lanes] = node
                else:
                    opener_total[rows, lanes] += node

        if b == 1:
            reduce_stage(2)
        for k in range(2):
            copy = pltpu.make_async_copy(
                regrets.at[b, k], new_river.at[0, b, :, k, :], out_sems.at[b, k]
            )
            copy.start()
            stores.append(copy)

    @pl.loop(0, L // STEP, unroll=True)
    def _(step):
        rows = rows_of(step)
        for lanes in GROUPS:
            top, rest = split(opener_total[rows, lanes])
            high[rows, lanes] = top
            low[rows, lanes] = rest
            top, rest = split(responder_total[rows, lanes] * strategy[rows, lanes])
            high[rows_of(step, L), lanes] = top
            low[rows_of(step, L), lanes] = rest

    flops = lax.broadcasted_iota(jnp.int32, (8, L), 0).astype(F32)
    for_opener = (flops == parents).astype(F32).astype(BF16)
    for_responder = (flops - F == parents).astype(F32).astype(BF16)
    nodes = (
        dot(for_opener, high[0:L, :])
        + dot(for_opener, low[0:L, :])
        + dot(for_responder, high[L : 2 * L, :])
        + dot(for_responder, low[L : 2 * L, :])
    )
    for i in range(8):
        parts[i] = nodes[i : i + 1, 0:HALF]
        parts[8 + i, :, 0 : HP - HALF] = nodes[i : i + 1, HALF:HP]
        parts[8 + i, :, HP - HALF :] = jnp.zeros((1, 2 * HALF - HP), F32)

    part_copies = [
        remote(parts.at[peer[1]], part_slots.at[d], part_send.at[d], part_recv.at[d], peer)
        for d, peer in enumerate(line_peers)
    ]
    start(part_copies)
    arrive(part_copies)
    total = parts[me]
    for d in range(Z - 1):
        total = total + part_slots[d]
    part_sum[...] = total
    all_nodes[me] = total
    plane_copies = [
        remote(part_sum, plane_slots.at[d], plane_send.at[d], plane_recv.at[d], peer)
        for d, peer in enumerate(plane_peers)
    ]
    node_copies = [
        remote(part_sum, all_nodes.at[me], node_send.at[d], node_recv.at[d], peer)
        for d, peer in enumerate(line_peers)
    ]
    start(plane_copies)
    start(node_copies)

    reduce_stage(3)
    arrive(plane_copies)
    for d in range(7):
        total = total + plane_slots[d]
    plane_sum[...] = total
    row_copies = [
        remote(plane_sum, row_slots.at[d], row_send.at[d], row_recv.at[d], peer)
        for d, peer in enumerate(row_peers)
    ]
    start(row_copies)
    arrive(row_copies)
    for d in range(3):
        total = total + row_slots[d]
    total = total * (1.0 / (32 * 32))
    final[...] = total
    finals[me] = total
    final_copies = [
        remote(final, finals.at[me], final_send.at[d], final_recv.at[d], peer)
        for d, peer in enumerate(line_peers)
    ]
    start(final_copies)

    arrive(node_copies)
    total = block_of(lines, me)[...]
    for way in range(2):
        nexts[way][-1].wait_recv()
        sums[way][-1].wait_recv()
        total = total + next_slots[way, STAGES - 1] + sum_slots[way, STAGES - 1]
    own = block_of(gathered, me)
    lane = lax.broadcasted_iota(jnp.int32, (1, L), 1)
    for i in range(OWN):
        mine = jnp.sum(
            jnp.where(lane == me * OWN + i, parents, 0.0), axis=1, keepdims=True
        )
        node_low, node_high = all_nodes[F], all_nodes[8 + F]
        for f in range(1, F):
            node_low = jnp.where(mine == f, all_nodes[F + f], node_low)
            node_high = jnp.where(mine == f, all_nodes[8 + F + f], node_high)
        new_turn[i, :, 0:HALF] = jnp.maximum(
            own[i, :, 0:HALF] + (total[i, :, 0:HALF] - node_low) * (1.0 / 32), 0.0
        )
        new_turn[i, :, HALF:H] = jnp.maximum(
            own[i, :, HALF:H]
            + (total[i, :, HALF:H] - node_high[:, 0 : H - HALF]) * (1.0 / 32),
            0.0,
        )

    arrive(final_copies)
    for i in range(8):
        player, f = i // F, i % F
        flop[player, f : f + 1, 0:HALF] = finals[i]
        flop[player, f : f + 1, HALF:H] = finals[8 + i][:, 0 : H - HALF]
    for copy in stores:
        copy.wait()
    for copy in (
        sum((stage for way in gathers for stage in way), [])
        + nexts[0]
        + nexts[1]
        + sums[0]
        + sums[1][1:]
        + part_copies
        + plane_copies
        + node_copies
        + row_copies
        + final_copies
    ):
        copy.wait_send()


def iterate(
    opener_reach,
    responder_reach,
    turn_parent,
    turn_cards,
    river_cards,
    showdown_ranks,
    fold_mask,
    half_pot,
    own,
    river_regrets,
):
    clear, counts, spreads, cards = tables()
    vmem = pl.BlockSpec(memory_space=pltpu.VMEM)
    hbm = pl.BlockSpec(memory_space=pltpu.HBM)
    dma = pltpu.SemaphoreType.DMA
    return pl.pallas_call(
        kernel,
        out_shape=(
            jax.ShapeDtypeStruct((OWN, 1, H), F32),
            jax.ShapeDtypeStruct(river_regrets.shape, F32),
            jax.ShapeDtypeStruct((2, F, H), F32),
        ),
        in_specs=[hbm] * 14,
        out_specs=(vmem, vmem, vmem),
        scratch_shapes=[
            pltpu.VMEM((F, H), F32),
            pltpu.VMEM((F, H), F32),
            pltpu.VMEM((1, L), jnp.int32),
            pltpu.VMEM((1, 1), jnp.int32),
            pltpu.VMEM((1, BOARDS), jnp.int32),
            pltpu.VMEM((1, BOARDS, H), jnp.int32),
            pltpu.VMEM((2, L), jnp.int32),
            pltpu.VMEM((2, L), F32),
            pltpu.VMEM((2 * HP, 128), BF16),
            pltpu.VMEM((256, HP), BF16),
            pltpu.VMEM((8, HP), jnp.int32),
            pltpu.VMEM((HP, HP), BF16),
            pltpu.VMEM((BOARDS, 2, L, H), F32),
            pltpu.VMEM((L, 1, H), F32),
            pltpu.VMEM((L, H), F32),
            pltpu.VMEM((BOARDS, HP, HP), BF16),
            pltpu.VMEM((BOARDS, L, H), F32),
            pltpu.VMEM((L, H), F32),
            pltpu.VMEM((L, H), F32),
            pltpu.VMEM((L, H), F32),
            pltpu.VMEM((3 * L, HP), BF16),
            pltpu.VMEM((3 * L, HP), BF16),
            pltpu.VMEM((3 * L, HP), F32),
            pltpu.VMEM((3 * L, HP), F32),
            pltpu.VMEM((5, L, 128), F32),
            pltpu.VMEM((BOARDS, STEP, HP), F32),
            pltpu.VMEM((8, HP), F32),
            pltpu.VMEM((BOARDS, HP, 128), F32),
            pltpu.VMEM((L, HP), F32),
            pltpu.VMEM((L, HP), F32),
            pltpu.VMEM((L, 1, HP), F32),
            pltpu.VMEM((Z, 1, HALF), F32),
            pltpu.VMEM((Z - 1, 1, HALF), F32),
            pltpu.VMEM((1, HALF), F32),
            pltpu.VMEM((Z, 1, HALF), F32),
            pltpu.VMEM((7, 1, HALF), F32),
            pltpu.VMEM((1, HALF), F32),
            pltpu.VMEM((3, 1, HALF), F32),
            pltpu.VMEM((1, HALF), F32),
            pltpu.VMEM((Z, 1, HALF), F32),
            pltpu.VMEM((2, STAGES, OWN, 1, HP), F32),
            pltpu.VMEM((2, STAGES, OWN, 1, HP), F32),
            pltpu.VMEM((2, STAGES - 1, OWN, 1, HP), F32),
            dma((11,)),
            dma,
            dma,
            dma((BOARDS, 2)),
            dma,
            dma((L // STEP,)),
            dma((BOARDS, 2)),
        ]
        + [
            dma(shape)
            for shape in (
                (2, STAGES, 2),
                (2, STAGES),
                (2, STAGES),
                (Z - 1,),
                (Z - 1,),
                (7,),
                (3,),
                (Z - 1,),
            )
            for _ in range(2)
        ],
        compiler_params=pltpu.CompilerParams(
            collective_id=0, has_side_effects=True, vmem_limit_bytes=46 * MIB
        ),
    )(
        *(
            pltpu.with_memory_space_constraint(operand, pltpu.HBM) if operand.size > 1 else operand
            for operand in (
                opener_reach,
                responder_reach,
                turn_parent.reshape(1, L),
                turn_cards.reshape(1, 1),
                river_cards,
                showdown_ranks,
                fold_mask.T,
                half_pot.T,
                jnp.asarray(counts),
                jnp.asarray(spreads),
                jnp.asarray(cards),
                jnp.asarray(clear),
                own,
                river_regrets,
            )
        )
    )


def on_device(
    opener_reach,
    responder_reach,
    turn_parent,
    turn_cards,
    river_cards,
    showdown_ranks,
    fold_mask,
    half_pot,
    turn_regrets,
    river_regrets,
):
    new_turn, new_river, flop_values = iterate(
        opener_reach,
        responder_reach,
        turn_parent,
        turn_cards,
        river_cards,
        showdown_ranks,
        fold_mask,
        half_pot,
        turn_regrets.reshape(OWN, 1, H),
        river_regrets,
    )
    return new_turn.reshape(1, OWN, H), new_river, flop_values


def solution(mesh):
    placed = (
        P(),
        P(),
        P(),
        P("turn"),
        P("turn", "river"),
        P("turn", "river", None),
        P(),
        P(),
        P("turn", "river", None),
        P("turn", "river", None, None, None),
    )
    return jax.shard_map(
        on_device,
        mesh=mesh,
        in_specs=placed,
        out_specs=(P("turn", "river", None), P("turn", "river", None, None, None), P()),
        check_vma=False,
    )
```

```python
import functools

import jax
import jax.numpy as jnp
import numpy as np
from jax import lax
from jax.experimental import pallas as pl
from jax.experimental.pallas import tpu as pltpu
from jax.sharding import PartitionSpec as P

MESH = pl.DeviceIdType.MESH
F32 = jnp.float32
BF16 = jnp.bfloat16

H = 1326
HP = 1408
L = 96
F = 4
Z = 16
OWN = L // Z
BOARDS = 2
HALF = 768
STEP = 16
STEPS = L // STEP
STAGES = Z // 4
MIB = 2**20
GROUPS = (slice(0, 512), slice(512, 1024), slice(1024, H))


def tables():
    low, high = np.triu_indices(52, 1)
    holds = np.zeros((HP, 64), np.float32)
    holds[np.arange(H), low] = 1.0
    holds[np.arange(H), high] = 1.0
    clear = (holds @ holds.T == 0).astype(np.float32)
    clear[H:] = 0.0
    clear[:, H:] = 0.0
    counts = holds.copy()
    counts[:H, 52] = 1.0
    spread = -holds.T.copy()
    spread[52, :H] = 1.0
    spreads = np.concatenate([spread, spread, spread, np.zeros_like(spread)], 0)
    cards = np.full((8, HP), -1, np.int32)
    cards[0, :H] = low
    cards[1, :H] = high
    return (
        clear.astype(BF16),
        np.tile(counts, (2, 2)).astype(BF16),
        spreads.astype(BF16),
        cards,
    )


def split(value):
    high = value.astype(BF16)
    return high, (value - high.astype(F32)).astype(BF16)


def dot(a, b):
    return jnp.dot(a, b, preferred_element_type=F32)


def column(row):
    return jnp.broadcast_to(row, (128, row.shape[1])).T


def wide(tile, lanes):
    width = lanes.stop - lanes.start
    return jnp.concatenate([tile] * (-(-width // 128)), 1)[:, :width]


def rows_of(step, start=0):
    if isinstance(step, int):
        return slice(step * STEP + start, step * STEP + start + STEP)
    return pl.ds(pl.multiple_of(step * STEP + start, STEP), STEP)


def kernel(
    opener_hbm,
    responder_hbm,
    parent_hbm,
    turn_card_hbm,
    river_cards_hbm,
    ranks_hbm,
    fold_hbm,
    pot_hbm,
    counts_hbm,
    spreads_hbm,
    cards_hbm,
    clear_hbm,
    own_hbm,
    river_hbm,
    new_turn,
    new_river,
    flop,
    opener_reach,
    responder_reach,
    parent_row,
    turn_card,
    river_cards,
    ranks,
    fold,
    pot,
    counts,
    spreads,
    cards,
    clear,
    regrets,
    gathered,
    turn_lines,
    signs,
    inverse,
    opener_lines,
    strategy,
    responder_lines,
    high,
    low,
    shown,
    free,
    columns,
    living,
    rank_rows,
    rank_columns,
    opener_total,
    responder_total,
    lines,
    parts,
    part_slots,
    part_sum,
    all_nodes,
    plane_slots,
    plane_sum,
    row_slots,
    final,
    finals,
    next_slots,
    sum_slots,
    sum_out,
    small_sems,
    clear_sem,
    own_sem,
    in_sems,
    turn_sem,
    line_sems,
    out_sems,
    gather_send,
    gather_recv,
    next_send,
    next_recv,
    sum_send,
    sum_recv,
    part_send,
    part_recv,
    node_send,
    node_recv,
    plane_send,
    plane_recv,
    row_send,
    row_recv,
    final_send,
    final_recv,
):
    me = lax.axis_index("river")
    turn = lax.axis_index("turn")
    row, place = turn // 8, lax.rem(turn, 8)

    def along(distance):
        return (turn, lax.rem(me + distance + Z, Z))

    line_peers = [along(d) for d in range(1, Z)]
    plane_peers = [(row * 8 + lax.rem(place + d, 8), me) for d in range(1, 8)]
    row_peers = [(lax.rem(row + d, 4) * 8 + place, me) for d in range(1, 4)]
    everyone = line_peers + plane_peers + row_peers
    barrier = pltpu.get_barrier_semaphore()
    for peer in everyone:
        pl.semaphore_signal(barrier, inc=1, device_id=peer, device_id_type=MESH)

    def block_of(ref, owner):
        return ref.at[pl.ds(lax.rem(owner + Z, Z) * OWN, OWN)]

    def remote(src, dst, send, recv, peer):
        return pltpu.make_async_remote_copy(
            src_ref=src,
            dst_ref=dst,
            send_sem=send,
            recv_sem=recv,
            device_id=peer,
            device_id_type=MESH,
        )

    def start(copies):
        for copy in copies:
            copy.start()

    def arrive(copies):
        for copy in copies:
            copy.wait_recv()

    own_load = pltpu.make_async_copy(own_hbm, block_of(gathered, me), own_sem)
    own_load.start()
    smalls = [
        pltpu.make_async_copy(src, dst, small_sems.at[i])
        for i, (src, dst) in enumerate(
            (
                (opener_hbm, opener_reach),
                (responder_hbm, responder_reach),
                (parent_hbm, parent_row),
                (turn_card_hbm, turn_card),
                (river_cards_hbm, river_cards),
                (ranks_hbm, ranks),
                (fold_hbm, fold),
                (pot_hbm, pot),
                (cards_hbm, cards),
                (counts_hbm, counts),
                (spreads_hbm, spreads),
            )
        )
    ]
    start(smalls)
    loads = [
        [
            pltpu.make_async_copy(
                river_hbm.at[0, b, :, k, :], regrets.at[b, k], in_sems.at[b, k]
            )
            for k in range(2)
        ]
        for b in range(BOARDS)
    ]
    clear_load = pltpu.make_async_copy(clear_hbm, clear, clear_sem)
    start(loads[0])
    clear_load.start()
    start(loads[1])
    gathers = [
        [
            [
                remote(
                    block_of(gathered, me - sign * 2 * stage),
                    block_of(gathered, me - sign * 2 * stage),
                    gather_send.at[way, stage, far],
                    gather_recv.at[way, stage, far],
                    along(sign * (1 + far)),
                )
                for far in range(1 if sign < 0 and stage == STAGES - 1 else 2)
            ]
            for stage in range(STAGES)
        ]
        for way, sign in enumerate((1, -1))
    ]

    def gather_stage(stage):
        for way in gathers:
            if stage:
                way[stage - 1][1].wait_recv()
            start(way[stage][::-1])

    def gather_end():
        for way in gathers:
            for stage in range(STAGES):
                way[stage][0].wait_recv()
        gathers[0][-1][1].wait_recv()

    own_load.wait()
    pl.semaphore_wait(barrier, len(everyone))
    gather_stage(0)
    for copy in smalls:
        copy.wait()

    parents = parent_row[...].astype(F32)
    columns[0] = column(parents)
    for k in range(2):
        folded = fold[k : k + 1, :].astype(F32)
        stake = pot[k : k + 1, :]
        columns[1 + k] = column(stake * (1.0 - folded))
        columns[3 + k] = column(stake * folded)
    for b in range(BOARDS):
        dead = jnp.zeros((1, HP), jnp.bool_)
        for card in (turn_card[...], river_cards[:, b : b + 1]):
            dead = dead | (cards[0:1, :] == card) | (cards[1:2, :] == card)
        living[b] = jnp.broadcast_to(jnp.where(dead, 0.0, 1.0).astype(F32), (STEP, HP))
    rank_rows[:, HP - 128 :] = jnp.zeros((8, 128), F32)
    rank_rows[0:BOARDS, 0:H] = ranks[0].astype(F32)
    high[:, HP - 128 :] = jnp.zeros((3 * L, 128), BF16)
    low[:, HP - 128 :] = jnp.zeros((3 * L, 128), BF16)
    responder_total[:, HP - 128 :] = jnp.zeros((L, 128), F32)
    for b in range(BOARDS):
        for c in range(HP // 128):
            tile = slice(c * 128, c * 128 + 128)
            rank_columns[b, tile, :] = column(rank_rows[b : b + 1, tile])

    def of_parent(reach, rows, lanes):
        parent = wide(columns[0, rows, :], lanes)
        line = jnp.broadcast_to(reach[0:1, lanes], parent.shape)
        for f in range(1, F):
            line = jnp.where(parent == f, reach[f : f + 1, lanes], line)
        return line

    @pl.loop(0, L // STEP, unroll=True)
    def _(step):
        rows = rows_of(step)
        for lanes in GROUPS:
            opener_lines[rows, lanes] = of_parent(opener_reach, rows, lanes)

    def free_of(b, begin, size):
        part = slice(begin, begin + size)
        per_card = dot(jnp.concatenate([high[part, :], low[part, :]], 1), counts[...])
        first = per_card.astype(BF16)
        rest = per_card - first.astype(F32)
        second = rest.astype(BF16)
        third = (rest - second.astype(F32)).astype(BF16)
        lane = lax.broadcasted_iota(jnp.int32, (size, 128), 1)
        left = jnp.where(lane < 64, first.astype(F32), second.astype(F32)).astype(BF16)
        free[b, 0:size, :] = dot(jnp.concatenate([left, third], 1), spreads[...])

    def sign_rows(b, rows):
        for lanes in (*GROUPS[:2], slice(1024, HP)):
            gap = rank_rows[b : b + 1, lanes] - wide(rank_columns[b, rows, :], lanes)
            sign = jnp.clip(gap, -1.0, 1.0).astype(BF16)
            signs[b, rows, lanes] = sign * clear[rows, lanes]

    def show(b, begin, size, beside=None):
        part = slice(begin, begin + size)
        for i, at in enumerate(range(0, HP, 256)):
            out = slice(at, min(at + 256, HP))
            shown[b, 0:size, out] = dot(high[part, :], signs[b, :, out])
            if beside is not None:
                beside(i)

    def sign_beside(b, step):
        count = HP // STEP

        @pl.loop(step * count // STEPS, (step + 1) * count // STEPS, unroll=True)
        def _(at):
            sign_rows(b, rows_of(at))

    def opener_ranges(b):
        for copy in loads[b]:
            copy.wait()

        @pl.loop(0, L // STEP, unroll=True)
        def _(step):
            rows = rows_of(step)
            for lanes in GROUPS:
                r0, r1 = regrets[b, 0, rows, lanes], regrets[b, 1, rows, lanes]
                inv = 1.0 / (r0 + r1)
                inverse[b, rows, lanes] = inv
                base = opener_lines[rows, lanes] * living[b, :, lanes] * inv
                for k, r in enumerate((r0, r1)):
                    top, rest = split(base * r)
                    high[rows_of(step, k * L), lanes] = top
                    low[rows_of(step, k * L), lanes] = rest

    def line_copy(step):
        rows = rows_of(step)
        return pltpu.make_async_copy(
            responder_total.at[rows], lines.at[rows, 0, :], line_sems.at[step]
        )

    def responder_values(b, step):
        rows = rows_of(step)
        for lanes in GROUPS:
            base = opener_lines[rows, lanes] * living[b, :, lanes] * inverse[b, rows, lanes]
            value = jnp.zeros(base.shape, F32)
            for k in range(2):
                line = rows_of(step, k * L)
                clean = free[b, line, lanes] + base * regrets[b, k, rows, lanes]
                value = value + wide(columns[1 + k, rows, :], lanes) * shown[b, line, lanes]
                value = value + wide(columns[3 + k, rows, :], lanes) * clean
            value = value * living[b, :, lanes]
            if b == 0:
                responder_total[rows, lanes] = value
            else:
                responder_total[rows, lanes] += value
        if b == 1:
            line_copy(step).start()

    clear_load.wait()

    @pl.loop(0, HP // STEP, unroll=True)
    def _(step):
        sign_rows(0, rows_of(step))

    gather_stage(1)
    opener_ranges(0)
    show(0, 0, 2 * L, functools.partial(sign_beside, 1))
    gather_stage(2)
    free_of(0, 0, 2 * L)
    opener_ranges(1)
    gather_stage(3)
    show(1, 0, 2 * L, functools.partial(responder_values, 0))
    free_of(1, 0, 2 * L)
    for step in range(STEPS):
        responder_values(1, step)

    nexts = [
        [
            remote(
                block_of(lines, me + sign * (7 - 2 * stage)),
                next_slots.at[way, stage],
                next_send.at[way, stage],
                next_recv.at[way, stage],
                along(sign),
            )
            for stage in range(STAGES)
        ]
        for way, sign in enumerate((1, -1))
    ]
    sums = [
        [
            remote(
                sum_out.at[way, stage - 1] if stage else block_of(lines, me + 8),
                sum_slots.at[way, stage],
                sum_send.at[way, stage],
                sum_recv.at[way, stage],
                along(2 * sign),
            )
            if stage or sign > 0
            else None
            for stage in range(STAGES)
        ]
        for way, sign in enumerate((1, -1))
    ]

    def reduce_stage(stage):
        for way, sign in enumerate((1, -1)):
            if stage:
                total = block_of(lines, me + sign * (8 - 2 * stage))[...]
                nexts[way][stage - 1].wait_recv()
                total = total + next_slots[way, stage - 1]
                if stage > 1 or sign > 0:
                    sums[way][stage - 1].wait_recv()
                    total = total + sum_slots[way, stage - 1]
                sum_out[way, stage - 1] = total
            if stage or sign > 0:
                sums[way][stage].start()
            nexts[way][stage].start()

    gather_end()
    turn_load = pltpu.make_async_copy(gathered.at[:, 0, :], turn_lines, turn_sem)
    turn_load.start()
    for step in range(STEPS):
        line_copy(step).wait()
    reduce_stage(0)

    turn_load.wait()

    @pl.loop(0, L // STEP, unroll=True)
    def _(step):
        rows = rows_of(step)
        for lanes in GROUPS:
            top, rest = split(turn_lines[rows, lanes])
            high[rows, lanes] = top
            low[rows, lanes] = rest

    same = (columns[0, :, 0:L] == parents).astype(F32).astype(BF16)
    shown[0, 0:L, :] = dot(same, high[0:L, :]) + dot(same, low[0:L, :])

    @pl.loop(0, L // STEP, unroll=True)
    def _(step):
        rows = rows_of(step)
        for lanes in GROUPS:
            share = turn_lines[rows, lanes] / shown[0, rows, lanes]
            strategy[rows, lanes] = share
            responder_lines[rows, lanes] = of_parent(responder_reach, rows, lanes) * share

    places = (2 * L, 0)

    def responder_ranges(b, step):
        rows = rows_of(step)
        line = rows_of(step, places[b])
        for lanes in GROUPS:
            top, rest = split(responder_lines[rows, lanes] * living[b, :, lanes])
            high[line, lanes] = top
            low[line, lanes] = rest

    def opener_values(b, step):
        rows = rows_of(step)
        for lanes in GROUPS:
            live = living[b, :, lanes]
            inv = inverse[b, rows, lanes]
            won = shown[b, rows, lanes] * live
            lost = (free[b, rows, lanes] + responder_lines[rows, lanes]) * live
            old, values = [], []
            node = jnp.zeros(live.shape, F32)
            for k in range(2):
                old.append(regrets[b, k, rows, lanes])
                values.append(
                    wide(columns[1 + k, rows, :], lanes) * won
                    - wide(columns[3 + k, rows, :], lanes) * lost
                )
                node = node + old[k] * inv * values[k]
            for k in range(2):
                regrets[b, k, rows, lanes] = jnp.maximum(old[k] + values[k] - node, 0.0)
            if b == 0:
                opener_total[rows, lanes] = node
            else:
                top, rest = split(opener_total[rows, lanes] + node)
                high[rows_of(step, 2 * L), lanes] = top
                low[rows_of(step, 2 * L), lanes] = rest

    def beside_first(step):
        responder_ranges(1, step)
        rows = rows_of(step)
        for lanes in GROUPS:
            top, rest = split(responder_total[rows, lanes] * strategy[rows, lanes])
            high[rows_of(step, L), lanes] = top
            low[rows_of(step, L), lanes] = rest

    def store(b):
        copies = [
            pltpu.make_async_copy(
                regrets.at[b, k], new_river.at[0, b, :, k, :], out_sems.at[b, k]
            )
            for k in range(2)
        ]
        start(copies)
        return copies

    for step in range(STEPS):
        responder_ranges(0, step)
    show(0, 2 * L, L, beside_first)
    free_of(0, 2 * L, L)
    reduce_stage(1)
    show(1, 0, L, functools.partial(opener_values, 0))
    free_of(1, 0, L)
    for step in range(STEPS):
        opener_values(1, step)

    flops = lax.broadcasted_iota(jnp.int32, (8, L), 0).astype(F32)
    for_opener = (flops == parents).astype(F32).astype(BF16)
    for_responder = (flops - F == parents).astype(F32).astype(BF16)
    nodes = (
        dot(for_opener, high[2 * L :, :])
        + dot(for_opener, low[2 * L :, :])
        + dot(for_responder, high[L : 2 * L, :])
        + dot(for_responder, low[L : 2 * L, :])
    )
    for i in range(8):
        parts[i] = nodes[i : i + 1, 0:HALF]
        parts[8 + i, :, 0 : HP - HALF] = nodes[i : i + 1, HALF:HP]
        parts[8 + i, :, HP - HALF :] = jnp.zeros((1, 2 * HALF - HP), F32)

    part_copies = [
        remote(parts.at[peer[1]], part_slots.at[d], part_send.at[d], part_recv.at[d], peer)
        for d, peer in enumerate(line_peers)
    ]
    start(part_copies)
    stores = store(0) + store(1)
    reduce_stage(2)
    arrive(part_copies)
    total = parts[me]
    for d in range(Z - 1):
        total = total + part_slots[d]
    part_sum[...] = total
    all_nodes[me] = total
    plane_copies = [
        remote(part_sum, plane_slots.at[d], plane_send.at[d], plane_recv.at[d], peer)
        for d, peer in enumerate(plane_peers)
    ]
    node_copies = [
        remote(part_sum, all_nodes.at[me], node_send.at[d], node_recv.at[d], peer)
        for d, peer in enumerate(line_peers)
    ]
    start(plane_copies)
    reduce_stage(3)
    for copy in (
        sum((stage for way in gathers for stage in way), []) + nexts[0][:3] + nexts[1][:3]
    ):
        copy.wait_send()

    arrive(plane_copies)
    for d in range(7):
        total = total + plane_slots[d]
    plane_sum[...] = total
    row_copies = [
        remote(plane_sum, row_slots.at[d], row_send.at[d], row_recv.at[d], peer)
        for d, peer in enumerate(row_peers)
    ]
    start(row_copies)
    start(node_copies)
    arrive(row_copies)
    for d in range(3):
        total = total + row_slots[d]
    total = total * (1.0 / (32 * 32))
    final[...] = total
    finals[me] = total
    final_copies = [
        remote(final, finals.at[me], final_send.at[d], final_recv.at[d], peer)
        for d, peer in enumerate(line_peers)
    ]
    start(final_copies)

    arrive(node_copies)
    total = block_of(lines, me)[...]
    for way in range(2):
        nexts[way][-1].wait_recv()
        sums[way][-1].wait_recv()
        total = total + next_slots[way, STAGES - 1] + sum_slots[way, STAGES - 1]
    own = block_of(gathered, me)
    lane = lax.broadcasted_iota(jnp.int32, (1, L), 1)
    for i in range(OWN):
        mine = jnp.sum(
            jnp.where(lane == me * OWN + i, parents, 0.0), axis=1, keepdims=True
        )
        node_low, node_high = all_nodes[F], all_nodes[8 + F]
        for f in range(1, F):
            node_low = jnp.where(mine == f, all_nodes[F + f], node_low)
            node_high = jnp.where(mine == f, all_nodes[8 + F + f], node_high)
        new_turn[i, :, 0:HALF] = jnp.maximum(
            own[i, :, 0:HALF] + (total[i, :, 0:HALF] - node_low) * (1.0 / 32), 0.0
        )
        new_turn[i, :, HALF:H] = jnp.maximum(
            own[i, :, HALF:H]
            + (total[i, :, HALF:H] - node_high[:, 0 : H - HALF]) * (1.0 / 32),
            0.0,
        )

    arrive(final_copies)
    for i in range(8):
        player, f = i // F, i % F
        flop[player, f : f + 1, 0:HALF] = finals[i]
        flop[player, f : f + 1, HALF:H] = finals[8 + i][:, 0 : H - HALF]
    for copy in stores:
        copy.wait()
    for copy in (
        nexts[0][3:]
        + nexts[1][3:]
        + sums[0]
        + sums[1][1:]
        + part_copies
        + plane_copies
        + node_copies
        + row_copies
        + final_copies
    ):
        copy.wait_send()


def iterate(
    opener_reach,
    responder_reach,
    turn_parent,
    turn_cards,
    river_cards,
    showdown_ranks,
    fold_mask,
    half_pot,
    own,
    river_regrets,
):
    clear, counts, spreads, cards = tables()
    vmem = pl.BlockSpec(memory_space=pltpu.VMEM)
    hbm = pl.BlockSpec(memory_space=pltpu.HBM)
    dma = pltpu.SemaphoreType.DMA
    return pl.pallas_call(
        kernel,
        out_shape=(
            jax.ShapeDtypeStruct((OWN, 1, H), F32),
            jax.ShapeDtypeStruct(river_regrets.shape, F32),
            jax.ShapeDtypeStruct((2, F, H), F32),
        ),
        in_specs=[hbm] * 14,
        out_specs=(vmem, vmem, vmem),
        scratch_shapes=[
            pltpu.VMEM((F, H), F32),
            pltpu.VMEM((F, H), F32),
            pltpu.VMEM((1, L), jnp.int32),
            pltpu.VMEM((1, 1), jnp.int32),
            pltpu.VMEM((1, BOARDS), jnp.int32),
            pltpu.VMEM((1, BOARDS, H), jnp.int32),
            pltpu.VMEM((2, L), jnp.int32),
            pltpu.VMEM((2, L), F32),
            pltpu.VMEM((2 * HP, 128), BF16),
            pltpu.VMEM((256, HP), BF16),
            pltpu.VMEM((8, HP), jnp.int32),
            pltpu.VMEM((HP, HP), BF16),
            pltpu.VMEM((BOARDS, 2, L, H), F32),
            pltpu.VMEM((L, 1, H), F32),
            pltpu.VMEM((L, H), F32),
            pltpu.VMEM((BOARDS, HP, HP), BF16),
            pltpu.VMEM((BOARDS, L, H), F32),
            pltpu.VMEM((L, H), F32),
            pltpu.VMEM((L, H), F32),
            pltpu.VMEM((L, H), F32),
            pltpu.VMEM((3 * L, HP), BF16),
            pltpu.VMEM((3 * L, HP), BF16),
            pltpu.VMEM((BOARDS, 2 * L, HP), F32),
            pltpu.VMEM((BOARDS, 2 * L, HP), F32),
            pltpu.VMEM((5, L, 128), F32),
            pltpu.VMEM((BOARDS, STEP, HP), F32),
            pltpu.VMEM((8, HP), F32),
            pltpu.VMEM((BOARDS, HP, 128), F32),
            pltpu.VMEM((L, HP), F32),
            pltpu.VMEM((L, HP), F32),
            pltpu.VMEM((L, 1, HP), F32),
            pltpu.VMEM((Z, 1, HALF), F32),
            pltpu.VMEM((Z - 1, 1, HALF), F32),
            pltpu.VMEM((1, HALF), F32),
            pltpu.VMEM((Z, 1, HALF), F32),
            pltpu.VMEM((7, 1, HALF), F32),
            pltpu.VMEM((1, HALF), F32),
            pltpu.VMEM((3, 1, HALF), F32),
            pltpu.VMEM((1, HALF), F32),
            pltpu.VMEM((Z, 1, HALF), F32),
            pltpu.VMEM((2, STAGES, OWN, 1, HP), F32),
            pltpu.VMEM((2, STAGES, OWN, 1, HP), F32),
            pltpu.VMEM((2, STAGES - 1, OWN, 1, HP), F32),
            dma((11,)),
            dma,
            dma,
            dma((BOARDS, 2)),
            dma,
            dma((L // STEP,)),
            dma((BOARDS, 2)),
        ]
        + [
            dma(shape)
            for shape in (
                (2, STAGES, 2),
                (2, STAGES),
                (2, STAGES),
                (Z - 1,),
                (Z - 1,),
                (7,),
                (3,),
                (Z - 1,),
            )
            for _ in range(2)
        ],
        compiler_params=pltpu.CompilerParams(
            collective_id=0, has_side_effects=True, vmem_limit_bytes=46 * MIB
        ),
    )(
        *(
            pltpu.with_memory_space_constraint(operand, pltpu.HBM) if operand.size > 1 else operand
            for operand in (
                opener_reach,
                responder_reach,
                turn_parent.reshape(1, L),
                turn_cards.reshape(1, 1),
                river_cards,
                showdown_ranks,
                fold_mask.T,
                half_pot.T,
                jnp.asarray(counts),
                jnp.asarray(spreads),
                jnp.asarray(cards),
                jnp.asarray(clear),
                own,
                river_regrets,
            )
        )
    )


def on_device(
    opener_reach,
    responder_reach,
    turn_parent,
    turn_cards,
    river_cards,
    showdown_ranks,
    fold_mask,
    half_pot,
    turn_regrets,
    river_regrets,
):
    new_turn, new_river, flop_values = iterate(
        opener_reach,
        responder_reach,
        turn_parent,
        turn_cards,
        river_cards,
        showdown_ranks,
        fold_mask,
        half_pot,
        turn_regrets.reshape(OWN, 1, H),
        river_regrets,
    )
    return new_turn.reshape(1, OWN, H), new_river, flop_values


def solution(mesh):
    placed = (
        P(),
        P(),
        P(),
        P("turn"),
        P("turn", "river"),
        P("turn", "river", None),
        P(),
        P(),
        P("turn", "river", None),
        P("turn", "river", None, None, None),
    )
    return jax.shard_map(
        on_device,
        mesh=mesh,
        in_specs=placed,
        out_specs=(P("turn", "river", None), P("turn", "river", None, None, None), P()),
        check_vma=False,
    )
```

```python
import functools

import jax
import jax.numpy as jnp
import numpy as np
from jax import lax
from jax.experimental import pallas as pl
from jax.experimental.pallas import tpu as pltpu
from jax.sharding import PartitionSpec as P

MESH = pl.DeviceIdType.MESH
F32 = jnp.float32
BF16 = jnp.bfloat16

H = 1326
HP = 1408
L = 96
F = 4
Z = 16
OWN = L // Z
BOARDS = 2
HALF = 768
STEP = 16
STEPS = L // STEP
STAGES = Z // 4
MIB = 2**20
GROUPS = (slice(0, 512), slice(512, 1024), slice(1024, H))


def tables():
    low, high = np.triu_indices(52, 1)
    holds = np.zeros((HP, 64), np.float32)
    holds[np.arange(H), low] = 1.0
    holds[np.arange(H), high] = 1.0
    clear = (holds @ holds.T == 0).astype(np.float32)
    clear[H:] = 0.0
    clear[:, H:] = 0.0
    counts = holds.copy()
    counts[:H, 52] = 1.0
    spread = -holds.T.copy()
    spread[52, :H] = 1.0
    spreads = np.concatenate([spread, spread, spread, np.zeros_like(spread)], 0)
    cards = np.full((8, HP), -1, np.int32)
    cards[0, :H] = low
    cards[1, :H] = high
    return (
        clear.astype(BF16),
        np.tile(counts, (2, 2)).astype(BF16),
        spreads.astype(BF16),
        cards,
    )


def split(value):
    high = value.astype(BF16)
    return high, (value - high.astype(F32)).astype(BF16)


def dot(a, b):
    return jnp.dot(a, b, preferred_element_type=F32)


def column(row):
    return jnp.broadcast_to(row, (128, row.shape[1])).T


def wide(tile, lanes):
    width = lanes.stop - lanes.start
    return jnp.concatenate([tile] * (-(-width // 128)), 1)[:, :width]


def rows_of(step, start=0):
    if isinstance(step, int):
        return slice(step * STEP + start, step * STEP + start + STEP)
    return pl.ds(pl.multiple_of(step * STEP + start, STEP), STEP)


def kernel(
    opener_hbm,
    responder_hbm,
    parent_hbm,
    turn_card_hbm,
    river_cards_hbm,
    ranks_hbm,
    fold_hbm,
    pot_hbm,
    counts_hbm,
    spreads_hbm,
    cards_hbm,
    clear_hbm,
    own_hbm,
    river_hbm,
    new_turn,
    new_river,
    flop,
    opener_reach,
    responder_reach,
    parent_row,
    turn_card,
    river_cards,
    ranks,
    fold,
    pot,
    counts,
    spreads,
    cards,
    clear,
    regrets,
    gathered,
    turn_lines,
    signs,
    inverse,
    opener_lines,
    strategy,
    responder_lines,
    high,
    low,
    shown,
    free,
    columns,
    living,
    rank_rows,
    rank_columns,
    opener_total,
    responder_total,
    lines,
    parts,
    part_slots,
    part_sum,
    all_nodes,
    plane_slots,
    plane_sum,
    row_slots,
    final,
    finals,
    next_slots,
    sum_slots,
    sum_out,
    small_sems,
    clear_sem,
    own_sem,
    in_sems,
    out_sems,
    gather_send,
    gather_recv,
    next_send,
    next_recv,
    sum_send,
    sum_recv,
    part_send,
    part_recv,
    node_send,
    node_recv,
    plane_send,
    plane_recv,
    row_send,
    row_recv,
    final_send,
    final_recv,
):
    me = lax.axis_index("river")
    turn = lax.axis_index("turn")
    row, place = turn // 8, lax.rem(turn, 8)

    def along(distance):
        return (turn, lax.rem(me + distance + Z, Z))

    line_peers = [along(d) for d in range(1, Z)]
    plane_peers = [(row * 8 + lax.rem(place + d, 8), me) for d in range(1, 8)]
    row_peers = [(lax.rem(row + d, 4) * 8 + place, me) for d in range(1, 4)]
    everyone = line_peers + plane_peers + row_peers
    barrier = pltpu.get_barrier_semaphore()
    for peer in everyone:
        pl.semaphore_signal(barrier, inc=1, device_id=peer, device_id_type=MESH)

    def block_of(ref, owner):
        return ref.at[lax.rem(owner + Z, Z)]

    def remote(src, dst, send, recv, peer):
        return pltpu.make_async_remote_copy(
            src_ref=src,
            dst_ref=dst,
            send_sem=send,
            recv_sem=recv,
            device_id=peer,
            device_id_type=MESH,
        )

    def start(copies):
        for copy in copies:
            copy.start()

    def arrive(copies):
        for copy in copies:
            copy.wait_recv()

    own_load = pltpu.make_async_copy(own_hbm.at[:, 0, :], block_of(gathered, me), own_sem)
    own_load.start()
    smalls = [
        pltpu.make_async_copy(src, dst, small_sems.at[i])
        for i, (src, dst) in enumerate(
            (
                (opener_hbm, opener_reach),
                (responder_hbm, responder_reach),
                (parent_hbm, parent_row),
                (turn_card_hbm, turn_card),
                (river_cards_hbm, river_cards),
                (ranks_hbm, ranks),
                (fold_hbm, fold),
                (pot_hbm, pot),
                (cards_hbm, cards),
                (counts_hbm, counts),
                (spreads_hbm, spreads),
            )
        )
    ]
    start(smalls)
    loads = [
        [
            pltpu.make_async_copy(
                river_hbm.at[0, b, :, k, :], regrets.at[b, k], in_sems.at[b, k]
            )
            for k in range(2)
        ]
        for b in range(BOARDS)
    ]
    clear_load = pltpu.make_async_copy(clear_hbm, clear, clear_sem)
    start(loads[0])
    clear_load.start()
    start(loads[1])
    gathers = [
        [
            [
                remote(
                    block_of(gathered, me - sign * 2 * stage) if stage else own_hbm.at[:, 0, :],
                    block_of(gathered, me - sign * 2 * stage),
                    gather_send.at[way, stage, far],
                    gather_recv.at[way, stage, far],
                    along(sign * (1 + far)),
                )
                for far in range(1 if sign < 0 and stage == STAGES - 1 else 2)
            ]
            for stage in range(STAGES)
        ]
        for way, sign in enumerate((1, -1))
    ]

    def gather_stage(stage):
        for way in gathers:
            if stage:
                way[stage - 1][1].wait_recv()
            start(way[stage][::-1])

    def gather_end():
        for way in gathers:
            for stage in range(STAGES):
                way[stage][0].wait_recv()
        gathers[0][-1][1].wait_recv()

    pl.semaphore_wait(barrier, len(everyone))
    gather_stage(0)
    for copy in [own_load] + smalls:
        copy.wait()

    parents = parent_row[...].astype(F32)
    columns[0] = column(parents)
    for k in range(2):
        folded = fold[k : k + 1, :].astype(F32)
        stake = pot[k : k + 1, :]
        columns[1 + k] = column(stake * (1.0 - folded))
        columns[3 + k] = column(stake * folded)
    for b in range(BOARDS):
        dead = jnp.zeros((1, HP), jnp.bool_)
        for card in (turn_card[...], river_cards[:, b : b + 1]):
            dead = dead | (cards[0:1, :] == card) | (cards[1:2, :] == card)
        living[b] = jnp.broadcast_to(jnp.where(dead, 0.0, 1.0).astype(F32), (STEP, HP))
    rank_rows[:, HP - 128 :] = jnp.zeros((8, 128), F32)
    rank_rows[0:BOARDS, 0:H] = ranks[0].astype(F32)
    high[:, HP - 128 :] = jnp.zeros((3 * L, 128), BF16)
    low[:, HP - 128 :] = jnp.zeros((3 * L, 128), BF16)
    responder_total[:, HP - 128 :] = jnp.zeros((L, 128), F32)
    for b in range(BOARDS):
        for c in range(HP // 128):
            tile = slice(c * 128, c * 128 + 128)
            rank_columns[b, tile, :] = column(rank_rows[b : b + 1, tile])

    def of_parent(reach, rows, lanes):
        parent = wide(columns[0, rows, :], lanes)
        line = jnp.broadcast_to(reach[0:1, lanes], parent.shape)
        for f in range(1, F):
            line = jnp.where(parent == f, reach[f : f + 1, lanes], line)
        return line

    @pl.loop(0, L // STEP, unroll=True)
    def _(step):
        rows = rows_of(step)
        for lanes in GROUPS:
            opener_lines[rows, lanes] = of_parent(opener_reach, rows, lanes)

    def free_of(b, begin, size):
        part = slice(begin, begin + size)
        per_card = dot(jnp.concatenate([high[part, :], low[part, :]], 1), counts[...])
        first = per_card.astype(BF16)
        rest = per_card - first.astype(F32)
        second = rest.astype(BF16)
        third = (rest - second.astype(F32)).astype(BF16)
        lane = lax.broadcasted_iota(jnp.int32, (size, 128), 1)
        left = jnp.where(lane < 64, first.astype(F32), second.astype(F32)).astype(BF16)
        free[b, 0:size, :] = dot(jnp.concatenate([left, third], 1), spreads[...])

    def sign_rows(b, rows):
        for lanes in (*GROUPS[:2], slice(1024, HP)):
            gap = rank_rows[b : b + 1, lanes] - wide(rank_columns[b, rows, :], lanes)
            sign = jnp.clip(gap, -1.0, 1.0).astype(BF16)
            signs[b, rows, lanes] = sign * clear[rows, lanes]

    def show(b, begin, size, beside=None):
        part = slice(begin, begin + size)
        for i, at in enumerate(range(0, HP, 256)):
            out = slice(at, min(at + 256, HP))
            shown[b, 0:size, out] = dot(high[part, :], signs[b, :, out])
            if beside is not None:
                beside(i)

    def sign_beside(b, step):
        count = HP // STEP

        @pl.loop(step * count // STEPS, (step + 1) * count // STEPS, unroll=True)
        def _(at):
            sign_rows(b, rows_of(at))

    def opener_ranges(b):
        for copy in loads[b]:
            copy.wait()

        @pl.loop(0, L // STEP, unroll=True)
        def _(step):
            rows = rows_of(step)
            for lanes in GROUPS:
                r0, r1 = regrets[b, 0, rows, lanes], regrets[b, 1, rows, lanes]
                inv = 1.0 / (r0 + r1)
                inverse[b, rows, lanes] = inv
                base = opener_lines[rows, lanes] * living[b, :, lanes] * inv
                for k, r in enumerate((r0, r1)):
                    top, rest = split(base * r)
                    high[rows_of(step, k * L), lanes] = top
                    low[rows_of(step, k * L), lanes] = rest

    def responder_values(b, step):
        rows = rows_of(step)
        for lanes in GROUPS:
            base = opener_lines[rows, lanes] * living[b, :, lanes] * inverse[b, rows, lanes]
            value = jnp.zeros(base.shape, F32)
            for k in range(2):
                line = rows_of(step, k * L)
                clean = free[b, line, lanes] + base * regrets[b, k, rows, lanes]
                value = value + wide(columns[1 + k, rows, :], lanes) * shown[b, line, lanes]
                value = value + wide(columns[3 + k, rows, :], lanes) * clean
            value = value * living[b, :, lanes]
            if b == 0:
                responder_total[rows, lanes] = value
            else:
                responder_total[rows, lanes] += value

    clear_load.wait()

    @pl.loop(0, HP // STEP, unroll=True)
    def _(step):
        sign_rows(0, rows_of(step))

    gather_stage(1)
    opener_ranges(0)
    show(0, 0, 2 * L, functools.partial(sign_beside, 1))
    gather_stage(2)
    free_of(0, 0, 2 * L)
    opener_ranges(1)
    gather_stage(3)
    show(1, 0, 2 * L, functools.partial(responder_values, 0))
    free_of(1, 0, 2 * L)
    for step in range(STEPS):
        responder_values(1, step)

    for owner in range(Z):
        lines[owner] = responder_total[owner * OWN : owner * OWN + OWN, :]

    nexts = [
        [
            remote(
                block_of(lines, me + sign * (7 - 2 * stage)),
                next_slots.at[way, stage],
                next_send.at[way, stage],
                next_recv.at[way, stage],
                along(sign),
            )
            for stage in range(STAGES)
        ]
        for way, sign in enumerate((1, -1))
    ]
    sums = [
        [
            remote(
                sum_out.at[way, stage - 1] if stage else block_of(lines, me + 8),
                sum_slots.at[way, stage],
                sum_send.at[way, stage],
                sum_recv.at[way, stage],
                along(2 * sign),
            )
            if stage or sign > 0
            else None
            for stage in range(STAGES)
        ]
        for way, sign in enumerate((1, -1))
    ]

    def reduce_stage(stage):
        for way, sign in enumerate((1, -1)):
            if stage:
                total = block_of(lines, me + sign * (8 - 2 * stage))[...]
                nexts[way][stage - 1].wait_recv()
                total = total + next_slots[way, stage - 1]
                if stage > 1 or sign > 0:
                    sums[way][stage - 1].wait_recv()
                    total = total + sum_slots[way, stage - 1]
                sum_out[way, stage - 1] = total
            if stage or sign > 0:
                sums[way][stage].start()
            nexts[way][stage].start()

    gather_end()
    reduce_stage(0)

    for owner in range(Z):
        turn_lines[owner * OWN : owner * OWN + OWN, :] = gathered[owner]

    @pl.loop(0, L // STEP, unroll=True)
    def _(step):
        rows = rows_of(step)
        for lanes in GROUPS:
            top, rest = split(turn_lines[rows, lanes])
            high[rows, lanes] = top
            low[rows, lanes] = rest

    same = (columns[0, :, 0:L] == parents).astype(F32).astype(BF16)
    shown[0, 0:L, :] = dot(same, high[0:L, :]) + dot(same, low[0:L, :])

    @pl.loop(0, L // STEP, unroll=True)
    def _(step):
        rows = rows_of(step)
        for lanes in GROUPS:
            share = turn_lines[rows, lanes] / shown[0, rows, lanes]
            strategy[rows, lanes] = share
            responder_lines[rows, lanes] = of_parent(responder_reach, rows, lanes) * share

    places = (2 * L, 0)

    def responder_ranges(b, step):
        rows = rows_of(step)
        line = rows_of(step, places[b])
        for lanes in GROUPS:
            top, rest = split(responder_lines[rows, lanes] * living[b, :, lanes])
            high[line, lanes] = top
            low[line, lanes] = rest

    def opener_values(b, step):
        rows = rows_of(step)
        for lanes in GROUPS:
            live = living[b, :, lanes]
            inv = inverse[b, rows, lanes]
            won = shown[b, rows, lanes] * live
            lost = (free[b, rows, lanes] + responder_lines[rows, lanes]) * live
            old, values = [], []
            node = jnp.zeros(live.shape, F32)
            for k in range(2):
                old.append(regrets[b, k, rows, lanes])
                values.append(
                    wide(columns[1 + k, rows, :], lanes) * won
                    - wide(columns[3 + k, rows, :], lanes) * lost
                )
                node = node + old[k] * inv * values[k]
            for k in range(2):
                regrets[b, k, rows, lanes] = jnp.maximum(old[k] + values[k] - node, 0.0)
            if b == 0:
                opener_total[rows, lanes] = node
            else:
                top, rest = split(opener_total[rows, lanes] + node)
                high[rows_of(step, 2 * L), lanes] = top
                low[rows_of(step, 2 * L), lanes] = rest

    def beside_first(step):
        responder_ranges(1, step)
        rows = rows_of(step)
        for lanes in GROUPS:
            top, rest = split(responder_total[rows, lanes] * strategy[rows, lanes])
            high[rows_of(step, L), lanes] = top
            low[rows_of(step, L), lanes] = rest

    def store(b):
        copies = [
            pltpu.make_async_copy(
                regrets.at[b, k], new_river.at[0, b, :, k, :], out_sems.at[b, k]
            )
            for k in range(2)
        ]
        start(copies)
        return copies

    for step in range(STEPS):
        responder_ranges(0, step)
    show(0, 2 * L, L, beside_first)
    free_of(0, 2 * L, L)
    reduce_stage(1)
    show(1, 0, L, functools.partial(opener_values, 0))
    free_of(1, 0, L)
    for step in range(STEPS):
        opener_values(1, step)

    flops = lax.broadcasted_iota(jnp.int32, (8, L), 0).astype(F32)
    for_opener = (flops == parents).astype(F32).astype(BF16)
    for_responder = (flops - F == parents).astype(F32).astype(BF16)
    nodes = (
        dot(for_opener, high[2 * L :, :])
        + dot(for_opener, low[2 * L :, :])
        + dot(for_responder, high[L : 2 * L, :])
        + dot(for_responder, low[L : 2 * L, :])
    )
    for i in range(8):
        parts[i] = nodes[i : i + 1, 0:HALF]
        parts[8 + i, :, 0 : HP - HALF] = nodes[i : i + 1, HALF:HP]
        parts[8 + i, :, HP - HALF :] = jnp.zeros((1, 2 * HALF - HP), F32)

    part_copies = [
        remote(parts.at[peer[1]], part_slots.at[d], part_send.at[d], part_recv.at[d], peer)
        for d, peer in enumerate(line_peers)
    ]
    start(part_copies)
    stores = store(0) + store(1)
    reduce_stage(2)
    arrive(part_copies)
    total = parts[me]
    for d in range(Z - 1):
        total = total + part_slots[d]
    part_sum[...] = total
    all_nodes[me] = total
    plane_copies = [
        remote(part_sum, plane_slots.at[d], plane_send.at[d], plane_recv.at[d], peer)
        for d, peer in enumerate(plane_peers)
    ]
    node_copies = [
        remote(part_sum, all_nodes.at[me], node_send.at[d], node_recv.at[d], peer)
        for d, peer in enumerate(line_peers)
    ]
    start(plane_copies)
    reduce_stage(3)
    for copy in (
        sum((stage for way in gathers for stage in way), []) + nexts[0][:3] + nexts[1][:3]
    ):
        copy.wait_send()

    arrive(plane_copies)
    for d in range(7):
        total = total + plane_slots[d]
    plane_sum[...] = total
    row_copies = [
        remote(plane_sum, row_slots.at[d], row_send.at[d], row_recv.at[d], peer)
        for d, peer in enumerate(row_peers)
    ]
    start(row_copies)
    start(node_copies)
    arrive(row_copies)
    for d in range(3):
        total = total + row_slots[d]
    total = total * (1.0 / (32 * 32))
    final[...] = total
    finals[me] = total
    final_copies = [
        remote(final, finals.at[me], final_send.at[d], final_recv.at[d], peer)
        for d, peer in enumerate(line_peers)
    ]
    start(final_copies)

    arrive(node_copies)
    total = block_of(lines, me)[...]
    for way in range(2):
        nexts[way][-1].wait_recv()
        sums[way][-1].wait_recv()
        total = total + next_slots[way, STAGES - 1] + sum_slots[way, STAGES - 1]
    own = block_of(gathered, me)[...]
    lane = lax.broadcasted_iota(jnp.int32, (1, L), 1)
    for i in range(OWN):
        mine = jnp.sum(
            jnp.where(lane == me * OWN + i, parents, 0.0), axis=1, keepdims=True
        )
        node_low, node_high = all_nodes[F], all_nodes[8 + F]
        for f in range(1, F):
            node_low = jnp.where(mine == f, all_nodes[F + f], node_low)
            node_high = jnp.where(mine == f, all_nodes[8 + F + f], node_high)
        new_turn[i, :, 0:HALF] = jnp.maximum(
            own[i : i + 1, 0:HALF] + (total[i : i + 1, 0:HALF] - node_low) * (1.0 / 32), 0.0
        )
        new_turn[i, :, HALF:H] = jnp.maximum(
            own[i : i + 1, HALF:H]
            + (total[i : i + 1, HALF:H] - node_high[:, 0 : H - HALF]) * (1.0 / 32),
            0.0,
        )

    arrive(final_copies)
    for i in range(8):
        player, f = i // F, i % F
        flop[player, f : f + 1, 0:HALF] = finals[i]
        flop[player, f : f + 1, HALF:H] = finals[8 + i][:, 0 : H - HALF]
    for copy in stores:
        copy.wait()
    for copy in (
        nexts[0][3:]
        + nexts[1][3:]
        + sums[0]
        + sums[1][1:]
        + part_copies
        + plane_copies
        + node_copies
        + row_copies
        + final_copies
    ):
        copy.wait_send()


def iterate(
    opener_reach,
    responder_reach,
    turn_parent,
    turn_cards,
    river_cards,
    showdown_ranks,
    fold_mask,
    half_pot,
    own,
    river_regrets,
):
    clear, counts, spreads, cards = tables()
    vmem = pl.BlockSpec(memory_space=pltpu.VMEM)
    hbm = pl.BlockSpec(memory_space=pltpu.HBM)
    dma = pltpu.SemaphoreType.DMA
    return pl.pallas_call(
        kernel,
        out_shape=(
            jax.ShapeDtypeStruct((OWN, 1, H), F32),
            jax.ShapeDtypeStruct(river_regrets.shape, F32),
            jax.ShapeDtypeStruct((2, F, H), F32),
        ),
        in_specs=[hbm] * 14,
        out_specs=(vmem, vmem, vmem),
        scratch_shapes=[
            pltpu.VMEM((F, H), F32),
            pltpu.VMEM((F, H), F32),
            pltpu.VMEM((1, L), jnp.int32),
            pltpu.VMEM((1, 1), jnp.int32),
            pltpu.VMEM((1, BOARDS), jnp.int32),
            pltpu.VMEM((1, BOARDS, H), jnp.int32),
            pltpu.VMEM((2, L), jnp.int32),
            pltpu.VMEM((2, L), F32),
            pltpu.VMEM((2 * HP, 128), BF16),
            pltpu.VMEM((256, HP), BF16),
            pltpu.VMEM((8, HP), jnp.int32),
            pltpu.VMEM((HP, HP), BF16),
            pltpu.VMEM((BOARDS, 2, L, H), F32),
            pltpu.VMEM((Z, OWN, H), F32),
            pltpu.VMEM((L, H), F32),
            pltpu.VMEM((BOARDS, HP, HP), BF16),
            pltpu.VMEM((BOARDS, L, H), F32),
            pltpu.VMEM((L, H), F32),
            pltpu.VMEM((L, H), F32),
            pltpu.VMEM((L, H), F32),
            pltpu.VMEM((3 * L, HP), BF16),
            pltpu.VMEM((3 * L, HP), BF16),
            pltpu.VMEM((BOARDS, 2 * L, HP), F32),
            pltpu.VMEM((BOARDS, 2 * L, HP), F32),
            pltpu.VMEM((5, L, 128), F32),
            pltpu.VMEM((BOARDS, STEP, HP), F32),
            pltpu.VMEM((8, HP), F32),
            pltpu.VMEM((BOARDS, HP, 128), F32),
            pltpu.VMEM((L, HP), F32),
            pltpu.VMEM((L, HP), F32),
            pltpu.VMEM((Z, OWN, HP), F32),
            pltpu.VMEM((Z, 1, HALF), F32),
            pltpu.VMEM((Z - 1, 1, HALF), F32),
            pltpu.VMEM((1, HALF), F32),
            pltpu.VMEM((Z, 1, HALF), F32),
            pltpu.VMEM((7, 1, HALF), F32),
            pltpu.VMEM((1, HALF), F32),
            pltpu.VMEM((3, 1, HALF), F32),
            pltpu.VMEM((1, HALF), F32),
            pltpu.VMEM((Z, 1, HALF), F32),
            pltpu.VMEM((2, STAGES, OWN, HP), F32),
            pltpu.VMEM((2, STAGES, OWN, HP), F32),
            pltpu.VMEM((2, STAGES - 1, OWN, HP), F32),
            dma((11,)),
            dma,
            dma,
            dma((BOARDS, 2)),
            dma((BOARDS, 2)),
        ]
        + [
            dma(shape)
            for shape in (
                (2, STAGES, 2),
                (2, STAGES),
                (2, STAGES),
                (Z - 1,),
                (Z - 1,),
                (7,),
                (3,),
                (Z - 1,),
            )
            for _ in range(2)
        ],
        compiler_params=pltpu.CompilerParams(
            collective_id=0, has_side_effects=True, vmem_limit_bytes=46 * MIB
        ),
    )(
        *(
            pltpu.with_memory_space_constraint(operand, pltpu.HBM) if operand.size > 1 else operand
            for operand in (
                opener_reach,
                responder_reach,
                turn_parent.reshape(1, L),
                turn_cards.reshape(1, 1),
                river_cards,
                showdown_ranks,
                fold_mask.T,
                half_pot.T,
                jnp.asarray(counts),
                jnp.asarray(spreads),
                jnp.asarray(cards),
                jnp.asarray(clear),
                own,
                river_regrets,
            )
        )
    )


def on_device(
    opener_reach,
    responder_reach,
    turn_parent,
    turn_cards,
    river_cards,
    showdown_ranks,
    fold_mask,
    half_pot,
    turn_regrets,
    river_regrets,
):
    new_turn, new_river, flop_values = iterate(
        opener_reach,
        responder_reach,
        turn_parent,
        turn_cards,
        river_cards,
        showdown_ranks,
        fold_mask,
        half_pot,
        turn_regrets.reshape(OWN, 1, H),
        river_regrets,
    )
    return new_turn.reshape(1, OWN, H), new_river, flop_values


def solution(mesh):
    placed = (
        P(),
        P(),
        P(),
        P("turn"),
        P("turn", "river"),
        P("turn", "river", None),
        P(),
        P(),
        P("turn", "river", None),
        P("turn", "river", None, None, None),
    )
    return jax.shard_map(
        on_device,
        mesh=mesh,
        in_specs=placed,
        out_specs=(P("turn", "river", None), P("turn", "river", None, None, None), P()),
        check_vma=False,
    )
```

```python
import functools

import jax
import jax.numpy as jnp
import numpy as np
from jax import lax
from jax.experimental import pallas as pl
from jax.experimental.pallas import tpu as pltpu
from jax.sharding import PartitionSpec as P

MESH = pl.DeviceIdType.MESH
F32 = jnp.float32
BF16 = jnp.bfloat16

H = 1326
HP = 1408
L = 96
F = 4
Z = 16
OWN = L // Z
BOARDS = 2
HALF = 768
STEP = 16
STEPS = L // STEP
STAGES = Z // 4
MIB = 2**20
GROUPS = (slice(0, 512), slice(512, 1024), slice(1024, H))


def tables():
    low, high = np.triu_indices(52, 1)
    holds = np.zeros((HP, 64), np.float32)
    holds[np.arange(H), low] = 1.0
    holds[np.arange(H), high] = 1.0
    clear = (holds @ holds.T == 0).astype(np.float32)
    clear[H:] = 0.0
    clear[:, H:] = 0.0
    counts = holds.copy()
    counts[:H, 52] = 1.0
    spread = -holds.T.copy()
    spread[52, :H] = 1.0
    spreads = np.concatenate([spread, spread, spread, np.zeros_like(spread)], 0)
    cards = np.full((8, HP), -1, np.int32)
    cards[0, :H] = low
    cards[1, :H] = high
    return (
        clear.astype(BF16),
        np.tile(counts, (2, 2)).astype(BF16),
        spreads.astype(BF16),
        cards,
    )


def split(value):
    high = value.astype(BF16)
    return high, (value - high.astype(F32)).astype(BF16)


def dot(a, b):
    return jnp.dot(a, b, preferred_element_type=F32)


def column(row):
    return jnp.broadcast_to(row, (128, row.shape[1])).T


def wide(tile, lanes):
    width = lanes.stop - lanes.start
    return jnp.concatenate([tile] * (-(-width // 128)), 1)[:, :width]


def rows_of(step, start=0):
    if isinstance(step, int):
        return slice(step * STEP + start, step * STEP + start + STEP)
    return pl.ds(pl.multiple_of(step * STEP + start, STEP), STEP)


def kernel(
    opener_hbm,
    responder_hbm,
    parent_hbm,
    turn_card_hbm,
    river_cards_hbm,
    ranks_hbm,
    fold_hbm,
    pot_hbm,
    counts_hbm,
    spreads_hbm,
    cards_hbm,
    clear_hbm,
    own_hbm,
    river_hbm,
    new_turn,
    new_river,
    flop,
    opener_reach,
    responder_reach,
    parent_row,
    turn_card,
    river_cards,
    ranks,
    fold,
    pot,
    counts,
    spreads,
    cards,
    clear,
    regrets,
    gathered,
    turn_lines,
    signs,
    inverse,
    opener_lines,
    strategy,
    responder_lines,
    high,
    low,
    shown,
    free,
    columns,
    living,
    rank_rows,
    rank_columns,
    opener_total,
    responder_total,
    lines,
    parts,
    part_slots,
    all_nodes,
    plane_slots,
    row_slots,
    finals,
    next_slots,
    sum_slots,
    sum_out,
    small_sems,
    clear_sem,
    own_sem,
    in_sems,
    turn_sem,
    line_sems,
    out_sems,
    gather_send,
    gather_recv,
    next_send,
    next_recv,
    sum_send,
    sum_recv,
    part_send,
    part_recv,
    node_send,
    node_recv,
    plane_send,
    plane_recv,
    row_send,
    row_recv,
    final_send,
    final_recv,
):
    me = lax.axis_index("river")
    turn = lax.axis_index("turn")
    row, place = turn // 8, lax.rem(turn, 8)

    def along(distance):
        return (turn, lax.rem(me + distance + Z, Z))

    distances = sorted(range(1, Z), key=lambda d: -min(d, Z - d))
    line_peers = [along(d) for d in distances]
    plane_peers = [(row * 8 + lax.rem(place + d, 8), me) for d in range(1, 8)]
    row_peers = [(lax.rem(row + d, 4) * 8 + place, me) for d in range(1, 4)]
    everyone = line_peers + plane_peers + row_peers
    barrier = pltpu.get_barrier_semaphore()
    for peer in everyone:
        pl.semaphore_signal(barrier, inc=1, device_id=peer, device_id_type=MESH)

    def block_of(ref, owner):
        return ref.at[pl.ds(lax.rem(owner + Z, Z) * OWN, OWN)]

    def remote(src, dst, send, recv, peer):
        return pltpu.make_async_remote_copy(
            src_ref=src,
            dst_ref=dst,
            send_sem=send,
            recv_sem=recv,
            device_id=peer,
            device_id_type=MESH,
        )

    def start(copies):
        for copy in copies:
            copy.start()

    def arrive(copies):
        for copy in copies:
            copy.wait_recv()

    own_load = pltpu.make_async_copy(own_hbm, block_of(gathered, me), own_sem)
    own_load.start()
    smalls = [
        pltpu.make_async_copy(src, dst, small_sems.at[i])
        for i, (src, dst) in enumerate(
            (
                (opener_hbm, opener_reach),
                (responder_hbm, responder_reach),
                (parent_hbm, parent_row),
                (turn_card_hbm, turn_card),
                (river_cards_hbm, river_cards),
                (ranks_hbm, ranks),
                (fold_hbm, fold),
                (pot_hbm, pot),
                (cards_hbm, cards),
                (counts_hbm, counts),
                (spreads_hbm, spreads),
            )
        )
    ]
    start(smalls)
    loads = [
        [
            pltpu.make_async_copy(
                river_hbm.at[0, b, :, k, :], regrets.at[b, k], in_sems.at[b, k]
            )
            for k in range(2)
        ]
        for b in range(BOARDS)
    ]
    clear_load = pltpu.make_async_copy(clear_hbm, clear, clear_sem)
    start(loads[0])
    clear_load.start()
    start(loads[1])
    gathers = [
        [
            [
                remote(
                    block_of(gathered, me - sign * 2 * stage) if stage else own_hbm,
                    block_of(gathered, me - sign * 2 * stage),
                    gather_send.at[way, stage, far],
                    gather_recv.at[way, stage, far],
                    along(sign * (1 + far)),
                )
                for far in range(1 if sign < 0 and stage == STAGES - 1 else 2)
            ]
            for stage in range(STAGES)
        ]
        for way, sign in enumerate((1, -1))
    ]

    def gather_stage(stage):
        for way in gathers:
            if stage:
                way[stage - 1][1].wait_recv()
            start(way[stage][::-1])

    def gather_end():
        for way in gathers:
            for stage in range(STAGES):
                way[stage][0].wait_recv()
        gathers[0][-1][1].wait_recv()

    pl.semaphore_wait(barrier, len(everyone))
    gather_stage(0)
    for copy in [own_load] + smalls:
        copy.wait()

    parents = parent_row[...].astype(F32)
    columns[0] = column(parents)
    for k in range(2):
        folded = fold[k : k + 1, :].astype(F32)
        stake = pot[k : k + 1, :]
        columns[1 + k] = column(stake * (1.0 - folded))
        columns[3 + k] = column(stake * folded)
    for b in range(BOARDS):
        dead = jnp.zeros((1, HP), jnp.bool_)
        for card in (turn_card[...], river_cards[:, b : b + 1]):
            dead = dead | (cards[0:1, :] == card) | (cards[1:2, :] == card)
        living[b] = jnp.broadcast_to(jnp.where(dead, 0.0, 1.0).astype(F32), (STEP, HP))
    rank_rows[:, HP - 128 :] = jnp.zeros((8, 128), F32)
    rank_rows[0:BOARDS, 0:H] = ranks[0].astype(F32)
    high[:, HP - 128 :] = jnp.zeros((3 * L, 128), BF16)
    low[:, HP - 128 :] = jnp.zeros((3 * L, 128), BF16)
    responder_total[:, HP - 128 :] = jnp.zeros((L, 128), F32)
    for b in range(BOARDS):
        for c in range(HP // 128):
            tile = slice(c * 128, c * 128 + 128)
            rank_columns[b, tile, :] = column(rank_rows[b : b + 1, tile])

    def of_parent(reach, rows, lanes):
        parent = wide(columns[0, rows, :], lanes)
        line = jnp.broadcast_to(reach[0:1, lanes], parent.shape)
        for f in range(1, F):
            line = jnp.where(parent == f, reach[f : f + 1, lanes], line)
        return line

    @pl.loop(0, L // STEP, unroll=True)
    def _(step):
        rows = rows_of(step)
        for lanes in GROUPS:
            opener_lines[rows, lanes] = of_parent(opener_reach, rows, lanes)

    def free_of(b, begin, size):
        part = slice(begin, begin + size)
        per_card = dot(jnp.concatenate([high[part, :], low[part, :]], 1), counts[...])
        first = per_card.astype(BF16)
        rest = per_card - first.astype(F32)
        second = rest.astype(BF16)
        third = (rest - second.astype(F32)).astype(BF16)
        lane = lax.broadcasted_iota(jnp.int32, (size, 128), 1)
        left = jnp.where(lane < 64, first.astype(F32), second.astype(F32)).astype(BF16)
        free[b, 0:size, :] = dot(jnp.concatenate([left, third], 1), spreads[...])

    def sign_rows(b, rows):
        for lanes in (*GROUPS[:2], slice(1024, HP)):
            gap = rank_rows[b : b + 1, lanes] - wide(rank_columns[b, rows, :], lanes)
            sign = jnp.clip(gap, -1.0, 1.0).astype(BF16)
            signs[b, rows, lanes] = sign * clear[rows, lanes]

    def show(b, begin, size, beside=None):
        part = slice(begin, begin + size)
        for i, at in enumerate(range(0, HP, 256)):
            out = slice(at, min(at + 256, HP))
            shown[b, 0:size, out] = dot(high[part, :], signs[b, :, out])
            if beside is not None:
                beside(i)

    def sign_beside(b, step):
        count = HP // STEP

        @pl.loop(step * count // STEPS, (step + 1) * count // STEPS, unroll=True)
        def _(at):
            sign_rows(b, rows_of(at))

    def opener_ranges(b):
        for copy in loads[b]:
            copy.wait()

        @pl.loop(0, L // STEP, unroll=True)
        def _(step):
            rows = rows_of(step)
            for lanes in GROUPS:
                r0, r1 = regrets[b, 0, rows, lanes], regrets[b, 1, rows, lanes]
                inv = 1.0 / (r0 + r1)
                inverse[b, rows, lanes] = inv
                base = opener_lines[rows, lanes] * living[b, :, lanes] * inv
                for k, r in enumerate((r0, r1)):
                    top, rest = split(base * r)
                    high[rows_of(step, k * L), lanes] = top
                    low[rows_of(step, k * L), lanes] = rest

    def line_copy(step):
        rows = rows_of(step)
        return pltpu.make_async_copy(
            responder_total.at[rows], lines.at[rows, 0, :], line_sems.at[step]
        )

    def responder_values(b, step):
        rows = rows_of(step)
        for lanes in GROUPS:
            base = opener_lines[rows, lanes] * living[b, :, lanes] * inverse[b, rows, lanes]
            value = jnp.zeros(base.shape, F32)
            for k in range(2):
                line = rows_of(step, k * L)
                clean = free[b, line, lanes] + base * regrets[b, k, rows, lanes]
                value = value + wide(columns[1 + k, rows, :], lanes) * shown[b, line, lanes]
                value = value + wide(columns[3 + k, rows, :], lanes) * clean
            value = value * living[b, :, lanes]
            if b == 0:
                responder_total[rows, lanes] = value
            else:
                responder_total[rows, lanes] += value
        if b == 1:
            line_copy(step).start()

    clear_load.wait()

    @pl.loop(0, HP // STEP, unroll=True)
    def _(step):
        sign_rows(0, rows_of(step))

    gather_stage(1)
    opener_ranges(0)
    show(0, 0, 2 * L, functools.partial(sign_beside, 1))
    gather_stage(2)
    free_of(0, 0, 2 * L)
    opener_ranges(1)
    gather_stage(3)
    show(1, 0, 2 * L, functools.partial(responder_values, 0))
    free_of(1, 0, 2 * L)
    for step in range(STEPS):
        responder_values(1, step)

    nexts = [
        [
            remote(
                block_of(lines, me + sign * (7 - 2 * stage)),
                next_slots.at[way, stage],
                next_send.at[way, stage],
                next_recv.at[way, stage],
                along(sign),
            )
            for stage in range(STAGES)
        ]
        for way, sign in enumerate((1, -1))
    ]
    sums = [
        [
            remote(
                sum_out.at[way, stage - 1] if stage else block_of(lines, me + 8),
                sum_slots.at[way, stage],
                sum_send.at[way, stage],
                sum_recv.at[way, stage],
                along(2 * sign),
            )
            if stage or sign > 0
            else None
            for stage in range(STAGES)
        ]
        for way, sign in enumerate((1, -1))
    ]

    def reduce_stage(stage):
        for way, sign in enumerate((1, -1)):
            if stage:
                total = block_of(lines, me + sign * (8 - 2 * stage))[...]
                nexts[way][stage - 1].wait_recv()
                total = total + next_slots[way, stage - 1]
                if stage > 1 or sign > 0:
                    sums[way][stage - 1].wait_recv()
                    total = total + sum_slots[way, stage - 1]
                sum_out[way, stage - 1] = total
            if stage or sign > 0:
                sums[way][stage].start()
            nexts[way][stage].start()

    gather_end()
    turn_load = pltpu.make_async_copy(gathered.at[:, 0, :], turn_lines, turn_sem)
    turn_load.start()
    for step in range(STEPS):
        line_copy(step).wait()
    reduce_stage(0)

    turn_load.wait()

    @pl.loop(0, L // STEP, unroll=True)
    def _(step):
        rows = rows_of(step)
        for lanes in GROUPS:
            top, rest = split(turn_lines[rows, lanes])
            high[rows, lanes] = top
            low[rows, lanes] = rest

    same = (columns[0, :, 0:L] == parents).astype(F32).astype(BF16)
    shown[0, 0:L, :] = dot(same, high[0:L, :]) + dot(same, low[0:L, :])

    @pl.loop(0, L // STEP, unroll=True)
    def _(step):
        rows = rows_of(step)
        for lanes in GROUPS:
            share = turn_lines[rows, lanes] / shown[0, rows, lanes]
            strategy[rows, lanes] = share
            responder_lines[rows, lanes] = of_parent(responder_reach, rows, lanes) * share

    places = (2 * L, 0)

    def responder_ranges(b, step):
        rows = rows_of(step)
        line = rows_of(step, places[b])
        for lanes in GROUPS:
            top, rest = split(responder_lines[rows, lanes] * living[b, :, lanes])
            high[line, lanes] = top
            low[line, lanes] = rest

    def opener_values(b, step):
        rows = rows_of(step)
        for lanes in GROUPS:
            live = living[b, :, lanes]
            inv = inverse[b, rows, lanes]
            won = shown[b, rows, lanes] * live
            lost = (free[b, rows, lanes] + responder_lines[rows, lanes]) * live
            old, values = [], []
            node = jnp.zeros(live.shape, F32)
            for k in range(2):
                old.append(regrets[b, k, rows, lanes])
                values.append(
                    wide(columns[1 + k, rows, :], lanes) * won
                    - wide(columns[3 + k, rows, :], lanes) * lost
                )
                node = node + old[k] * inv * values[k]
            for k in range(2):
                regrets[b, k, rows, lanes] = jnp.maximum(old[k] + values[k] - node, 0.0)
            if b == 0:
                opener_total[rows, lanes] = node
            else:
                top, rest = split(opener_total[rows, lanes] + node)
                high[rows_of(step, 2 * L), lanes] = top
                low[rows_of(step, 2 * L), lanes] = rest

    def beside_first(step):
        responder_ranges(1, step)
        rows = rows_of(step)
        for lanes in GROUPS:
            top, rest = split(responder_total[rows, lanes] * strategy[rows, lanes])
            high[rows_of(step, L), lanes] = top
            low[rows_of(step, L), lanes] = rest

    def store(b):
        copies = [
            pltpu.make_async_copy(
                regrets.at[b, k], new_river.at[0, b, :, k, :], out_sems.at[b, k]
            )
            for k in range(2)
        ]
        start(copies)
        return copies

    for step in range(STEPS):
        responder_ranges(0, step)
    show(0, 2 * L, L, beside_first)
    free_of(0, 2 * L, L)
    reduce_stage(1)
    show(1, 0, L, functools.partial(opener_values, 0))
    stores = store(0)
    free_of(1, 0, L)
    for step in range(STEPS):
        opener_values(1, step)

    flops = lax.broadcasted_iota(jnp.int32, (8, L), 0).astype(F32)
    for_opener = (flops == parents).astype(F32).astype(BF16)
    for_responder = (flops - F == parents).astype(F32).astype(BF16)
    nodes = (
        dot(for_opener, high[2 * L :, :])
        + dot(for_opener, low[2 * L :, :])
        + dot(for_responder, high[L : 2 * L, :])
        + dot(for_responder, low[L : 2 * L, :])
    )
    for i in range(8):
        parts[i] = nodes[i : i + 1, 0:HALF]
        parts[8 + i, :, 0 : HP - HALF] = nodes[i : i + 1, HALF:HP]
        parts[8 + i, :, HP - HALF :] = jnp.zeros((1, 2 * HALF - HP), F32)

    def exchange(src_of, slots, semaphores, offsets, peers):
        send, recv = semaphores
        copies = [
            remote(src_of(peer), slots.at[d], send, recv, peer)
            for d, peer in zip(offsets, peers)
        ]
        start(copies)

    def landed(slots, semaphores):
        pltpu.make_async_copy(
            slots.at[pl.ds(1, slots.shape[0] - 1)],
            slots.at[pl.ds(1, slots.shape[0] - 1)],
            semaphores[1],
        ).wait()

    def sent(slots, semaphores):
        pltpu.make_async_copy(
            slots.at[pl.ds(1, slots.shape[0] - 1)],
            slots.at[pl.ds(1, slots.shape[0] - 1)],
            semaphores[0],
        ).wait()

    def sum_of(slots):
        total = slots[0]
        for d in range(1, slots.shape[0]):
            total = total + slots[d]
        return total

    part_sems = (part_send, part_recv)
    plane_sems = (plane_send, plane_recv)
    row_sems = (row_send, row_recv)
    node_sems = (node_send, node_recv)
    final_sems = (final_send, final_recv)
    exchange(lambda peer: parts.at[peer[1]], part_slots, part_sems, distances, line_peers)
    part_slots[0] = parts[me]
    reduce_stage(2)
    landed(part_slots, part_sems)
    total = sum_of(part_slots)
    plane_slots[0] = total
    all_nodes[0] = total
    exchange(lambda peer: plane_slots.at[0], plane_slots, plane_sems, range(1, 8), plane_peers)
    reduce_stage(3)
    for copy in (
        sum((stage for way in gathers for stage in way), []) + nexts[0][:3] + nexts[1][:3]
    ):
        copy.wait_send()

    landed(plane_slots, plane_sems)
    row_slots[0] = sum_of(plane_slots)
    exchange(lambda peer: row_slots.at[0], row_slots, row_sems, range(1, 4), row_peers)
    exchange(lambda peer: all_nodes.at[0], all_nodes, node_sems, distances, line_peers)
    landed(row_slots, row_sems)
    finals[0] = sum_of(row_slots) * (1.0 / (32 * 32))
    exchange(lambda peer: finals.at[0], finals, final_sems, distances, line_peers)
    stores = stores + store(1)

    def chunk(slots, at):
        return slots[lax.rem(me - at + Z, Z)]

    landed(all_nodes, node_sems)
    total = block_of(lines, me)[...]
    for way in range(2):
        nexts[way][-1].wait_recv()
        sums[way][-1].wait_recv()
        total = total + next_slots[way, STAGES - 1] + sum_slots[way, STAGES - 1]
    own = block_of(gathered, me)
    lane = lax.broadcasted_iota(jnp.int32, (1, L), 1)
    for i in range(OWN):
        mine = jnp.sum(
            jnp.where(lane == me * OWN + i, parents, 0.0), axis=1, keepdims=True
        )
        node_low, node_high = chunk(all_nodes, F), chunk(all_nodes, 8 + F)
        for f in range(1, F):
            node_low = jnp.where(mine == f, chunk(all_nodes, F + f), node_low)
            node_high = jnp.where(mine == f, chunk(all_nodes, 8 + F + f), node_high)
        new_turn[i, :, 0:HALF] = jnp.maximum(
            own[i, :, 0:HALF] + (total[i, :, 0:HALF] - node_low) * (1.0 / 32), 0.0
        )
        new_turn[i, :, HALF:H] = jnp.maximum(
            own[i, :, HALF:H]
            + (total[i, :, HALF:H] - node_high[:, 0 : H - HALF]) * (1.0 / 32),
            0.0,
        )

    landed(finals, final_sems)
    for i in range(8):
        player, f = i // F, i % F
        flop[player, f : f + 1, 0:HALF] = chunk(finals, i)
        flop[player, f : f + 1, HALF:H] = chunk(finals, 8 + i)[:, 0 : H - HALF]
    for copy in stores:
        copy.wait()
    for copy in nexts[0][3:] + nexts[1][3:] + sums[0] + sums[1][1:]:
        copy.wait_send()
    sent(part_slots, part_sems)
    sent(plane_slots, plane_sems)
    sent(row_slots, row_sems)
    sent(all_nodes, node_sems)
    sent(finals, final_sems)


def iterate(
    opener_reach,
    responder_reach,
    turn_parent,
    turn_cards,
    river_cards,
    showdown_ranks,
    fold_mask,
    half_pot,
    own,
    river_regrets,
):
    clear, counts, spreads, cards = tables()
    vmem = pl.BlockSpec(memory_space=pltpu.VMEM)
    hbm = pl.BlockSpec(memory_space=pltpu.HBM)
    dma = pltpu.SemaphoreType.DMA
    return pl.pallas_call(
        kernel,
        out_shape=(
            jax.ShapeDtypeStruct((OWN, 1, H), F32),
            jax.ShapeDtypeStruct(river_regrets.shape, F32),
            jax.ShapeDtypeStruct((2, F, H), F32),
        ),
        in_specs=[hbm] * 14,
        out_specs=(vmem, vmem, vmem),
        scratch_shapes=[
            pltpu.VMEM((F, H), F32),
            pltpu.VMEM((F, H), F32),
            pltpu.VMEM((1, L), jnp.int32),
            pltpu.VMEM((1, 1), jnp.int32),
            pltpu.VMEM((1, BOARDS), jnp.int32),
            pltpu.VMEM((1, BOARDS, H), jnp.int32),
            pltpu.VMEM((2, L), jnp.int32),
            pltpu.VMEM((2, L), F32),
            pltpu.VMEM((2 * HP, 128), BF16),
            pltpu.VMEM((256, HP), BF16),
            pltpu.VMEM((8, HP), jnp.int32),
            pltpu.VMEM((HP, HP), BF16),
            pltpu.VMEM((BOARDS, 2, L, H), F32),
            pltpu.VMEM((L, 1, H), F32),
            pltpu.VMEM((L, H), F32),
            pltpu.VMEM((BOARDS, HP, HP), BF16),
            pltpu.VMEM((BOARDS, L, H), F32),
            pltpu.VMEM((L, H), F32),
            pltpu.VMEM((L, H), F32),
            pltpu.VMEM((L, H), F32),
            pltpu.VMEM((3 * L, HP), BF16),
            pltpu.VMEM((3 * L, HP), BF16),
            pltpu.VMEM((BOARDS, 2 * L, HP), F32),
            pltpu.VMEM((BOARDS, 2 * L, HP), F32),
            pltpu.VMEM((5, L, 128), F32),
            pltpu.VMEM((BOARDS, STEP, HP), F32),
            pltpu.VMEM((8, HP), F32),
            pltpu.VMEM((BOARDS, HP, 128), F32),
            pltpu.VMEM((L, HP), F32),
            pltpu.VMEM((L, HP), F32),
            pltpu.VMEM((L, 1, HP), F32),
            pltpu.VMEM((Z, 1, HALF), F32),
            pltpu.VMEM((Z, 1, HALF), F32),
            pltpu.VMEM((Z, 1, HALF), F32),
            pltpu.VMEM((8, 1, HALF), F32),
            pltpu.VMEM((4, 1, HALF), F32),
            pltpu.VMEM((Z, 1, HALF), F32),
            pltpu.VMEM((2, STAGES, OWN, 1, HP), F32),
            pltpu.VMEM((2, STAGES, OWN, 1, HP), F32),
            pltpu.VMEM((2, STAGES - 1, OWN, 1, HP), F32),
            dma((11,)),
            dma,
            dma,
            dma((BOARDS, 2)),
            dma,
            dma((L // STEP,)),
            dma((BOARDS, 2)),
        ]
        + [
            dma(shape)
            for shape in ((2, STAGES, 2), (2, STAGES), (2, STAGES))
            for _ in range(2)
        ]
        + [dma] * 10,
        compiler_params=pltpu.CompilerParams(
            collective_id=0, has_side_effects=True, vmem_limit_bytes=46 * MIB
        ),
    )(
        *(
            pltpu.with_memory_space_constraint(operand, pltpu.HBM) if operand.size > 1 else operand
            for operand in (
                opener_reach,
                responder_reach,
                turn_parent.reshape(1, L),
                turn_cards.reshape(1, 1),
                river_cards,
                showdown_ranks,
                fold_mask.T,
                half_pot.T,
                jnp.asarray(counts),
                jnp.asarray(spreads),
                jnp.asarray(cards),
                jnp.asarray(clear),
                own,
                river_regrets,
            )
        )
    )


def on_device(
    opener_reach,
    responder_reach,
    turn_parent,
    turn_cards,
    river_cards,
    showdown_ranks,
    fold_mask,
    half_pot,
    turn_regrets,
    river_regrets,
):
    new_turn, new_river, flop_values = iterate(
        opener_reach,
        responder_reach,
        turn_parent,
        turn_cards,
        river_cards,
        showdown_ranks,
        fold_mask,
        half_pot,
        turn_regrets.reshape(OWN, 1, H),
        river_regrets,
    )
    return new_turn.reshape(1, OWN, H), new_river, flop_values


def solution(mesh):
    placed = (
        P(),
        P(),
        P(),
        P("turn"),
        P("turn", "river"),
        P("turn", "river", None),
        P(),
        P(),
        P("turn", "river", None),
        P("turn", "river", None, None, None),
    )
    return jax.shard_map(
        on_device,
        mesh=mesh,
        in_specs=placed,
        out_specs=(P("turn", "river", None), P("turn", "river", None, None, None), P()),
        check_vma=False,
    )
```

```python
import functools

import jax
import jax.numpy as jnp
import numpy as np
from jax import lax
from jax.experimental import pallas as pl
from jax.experimental.pallas import tpu as pltpu
from jax.sharding import PartitionSpec as P

MESH = pl.DeviceIdType.MESH
F32 = jnp.float32
BF16 = jnp.bfloat16

H = 1326
HP = 1408
L = 96
F = 4
Z = 16
OWN = L // Z
BOARDS = 2
HALF = 768
STEP = 16
STEPS = L // STEP
PIECES = 8
STAGES = Z // 4
MIB = 2**20
GROUPS = (slice(0, 512), slice(512, 1024), slice(1024, H))


def tables():
    low, high = np.triu_indices(52, 1)
    holds = np.zeros((HP, 64), np.float32)
    holds[np.arange(H), low] = 1.0
    holds[np.arange(H), high] = 1.0
    clear = (holds @ holds.T == 0).astype(np.float32)
    clear[H:] = 0.0
    clear[:, H:] = 0.0
    counts = holds.copy()
    counts[:H, 52] = 1.0
    spread = -holds.T.copy()
    spread[52, :H] = 1.0
    spreads = np.concatenate([spread, spread, spread, np.zeros_like(spread)], 0)
    cards = np.full((8, HP), -1, np.int32)
    cards[0, :H] = low
    cards[1, :H] = high
    return (
        clear.astype(BF16),
        np.tile(counts, (2, 2)).astype(BF16),
        spreads.astype(BF16),
        cards,
    )


def split(value):
    high = value.astype(BF16)
    return high, (value - high.astype(F32)).astype(BF16)


def dot(a, b):
    return jnp.dot(a, b, preferred_element_type=F32)


def column(row):
    return jnp.broadcast_to(row, (128, row.shape[1])).T


def wide(tile, lanes):
    width = lanes.stop - lanes.start
    return jnp.concatenate([tile] * (-(-width // 128)), 1)[:, :width]


def rows_of(step, start=0):
    if isinstance(step, int):
        return slice(step * STEP + start, step * STEP + start + STEP)
    return pl.ds(pl.multiple_of(step * STEP + start, STEP), STEP)


def kernel(
    opener_hbm,
    responder_hbm,
    parent_hbm,
    turn_card_hbm,
    river_cards_hbm,
    ranks_hbm,
    fold_hbm,
    pot_hbm,
    counts_hbm,
    spreads_hbm,
    cards_hbm,
    clear_hbm,
    own_hbm,
    river_hbm,
    new_turn,
    new_river,
    flop,
    opener_reach,
    responder_reach,
    parent_row,
    turn_card,
    river_cards,
    ranks,
    fold,
    pot,
    counts,
    spreads,
    cards,
    clear,
    regrets,
    gathered,
    turn_lines,
    signs,
    inverse,
    opener_lines,
    strategy,
    responder_lines,
    high,
    low,
    shown,
    free,
    columns,
    living,
    rank_rows,
    rank_columns,
    opener_total,
    responder_total,
    lines,
    parts,
    part_slots,
    all_nodes,
    plane_slots,
    row_slots,
    finals,
    next_slots,
    sum_slots,
    sum_out,
    small_sems,
    clear_sems,
    own_sem,
    in_sems,
    turn_sem,
    line_sems,
    out_sems,
    gather_send,
    gather_recv,
    next_send,
    next_recv,
    sum_send,
    sum_recv,
    part_send,
    part_recv,
    node_send,
    node_recv,
    plane_send,
    plane_recv,
    row_send,
    row_recv,
    final_send,
    final_recv,
):
    me = lax.axis_index("river")
    turn = lax.axis_index("turn")
    row, place = turn // 8, lax.rem(turn, 8)

    def along(distance):
        return (turn, lax.rem(me + distance + Z, Z))

    distances = sorted(range(1, Z), key=lambda d: -min(d, Z - d))
    line_peers = [along(d) for d in distances]
    plane_peers = [(row * 8 + lax.rem(place + d, 8), me) for d in range(1, 8)]
    row_peers = [(lax.rem(row + d, 4) * 8 + place, me) for d in range(1, 4)]
    everyone = line_peers + plane_peers + row_peers
    barrier = pltpu.get_barrier_semaphore()
    for peer in everyone:
        pl.semaphore_signal(barrier, inc=1, device_id=peer, device_id_type=MESH)

    def block_of(ref, owner):
        return ref.at[pl.ds(lax.rem(owner + Z, Z) * OWN, OWN)]

    def remote(src, dst, send, recv, peer):
        return pltpu.make_async_remote_copy(
            src_ref=src,
            dst_ref=dst,
            send_sem=send,
            recv_sem=recv,
            device_id=peer,
            device_id_type=MESH,
        )

    def start(copies):
        for copy in copies:
            copy.start()

    def arrive(copies):
        for copy in copies:
            copy.wait_recv()

    own_load = pltpu.make_async_copy(own_hbm, block_of(gathered, me), own_sem)
    own_load.start()
    smalls = [
        pltpu.make_async_copy(src, dst, small_sems.at[i])
        for i, (src, dst) in enumerate(
            (
                (opener_hbm, opener_reach),
                (responder_hbm, responder_reach),
                (parent_hbm, parent_row),
                (turn_card_hbm, turn_card),
                (river_cards_hbm, river_cards),
                (ranks_hbm, ranks),
                (fold_hbm, fold),
                (pot_hbm, pot),
                (cards_hbm, cards),
                (counts_hbm, counts),
                (spreads_hbm, spreads),
            )
        )
    ]
    start(smalls[:-2])
    loads = [
        [
            pltpu.make_async_copy(
                river_hbm.at[0, b, :, k, :], regrets.at[b, k], in_sems.at[b, k]
            )
            for k in range(2)
        ]
        for b in range(BOARDS)
    ]
    pieces = [pl.ds(i * (HP // PIECES), HP // PIECES) for i in range(PIECES)]
    clear_loads = [
        pltpu.make_async_copy(clear_hbm.at[piece], clear.at[piece], clear_sems.at[i])
        for i, piece in enumerate(pieces)
    ]
    start(clear_loads)
    start(loads[0])
    start(smalls[-2:])
    start(loads[1])
    def half_of(owner, half):
        first = lax.rem(owner + Z, Z) * OWN + half * (OWN // 2)
        return gathered.at[pl.ds(first, OWN // 2)]

    gathers = [
        [
            [
                [
                    remote(
                        half_of(me - sign * 2 * stage, half)
                        if stage
                        else own_hbm.at[pl.ds(half * (OWN // 2), OWN // 2)],
                        half_of(me - sign * 2 * stage, half),
                        gather_send.at[way, half, stage, far],
                        gather_recv.at[way, half, stage, far],
                        along(sign * (1 + far)),
                    )
                    for far in range(1 if sign < 0 and stage == STAGES - 1 else 2)
                ]
                for stage in range(STAGES)
            ]
            for half in range(2)
        ]
        for way, sign in enumerate((1, -1))
    ]

    def gather_stage(stage):
        for half in range(2):
            for way in gathers:
                if stage:
                    way[half][stage - 1][1].wait_recv()
                start(way[half][stage][::-1])

    def gather_end():
        for way in gathers:
            for half in range(2):
                for stage in range(STAGES):
                    way[half][stage][0].wait_recv()
        for half in range(2):
            gathers[0][half][-1][1].wait_recv()

    pl.semaphore_wait(barrier, len(everyone))
    gather_stage(0)
    for copy in [own_load] + smalls[:-2]:
        copy.wait()

    parents = parent_row[...].astype(F32)
    columns[0] = column(parents)
    for k in range(2):
        folded = fold[k : k + 1, :].astype(F32)
        stake = pot[k : k + 1, :]
        columns[1 + k] = column(stake * (1.0 - folded))
        columns[3 + k] = column(stake * folded)
    for b in range(BOARDS):
        dead = jnp.zeros((1, HP), jnp.bool_)
        for card in (turn_card[...], river_cards[:, b : b + 1]):
            dead = dead | (cards[0:1, :] == card) | (cards[1:2, :] == card)
        living[b] = jnp.broadcast_to(jnp.where(dead, 0.0, 1.0).astype(F32), (STEP, HP))
    rank_rows[:, HP - 128 :] = jnp.zeros((8, 128), F32)
    rank_rows[0:BOARDS, 0:H] = ranks[0].astype(F32)
    high[:, HP - 128 :] = jnp.zeros((3 * L, 128), BF16)
    low[:, HP - 128 :] = jnp.zeros((3 * L, 128), BF16)
    responder_total[:, HP - 128 :] = jnp.zeros((L, 128), F32)
    for b in range(BOARDS):
        for c in range(HP // 128):
            tile = slice(c * 128, c * 128 + 128)
            rank_columns[b, tile, :] = column(rank_rows[b : b + 1, tile])

    def of_parent(reach, rows, lanes):
        parent = wide(columns[0, rows, :], lanes)
        line = jnp.broadcast_to(reach[0:1, lanes], parent.shape)
        for f in range(1, F):
            line = jnp.where(parent == f, reach[f : f + 1, lanes], line)
        return line

    @pl.loop(0, L // STEP, unroll=True)
    def _(step):
        rows = rows_of(step)
        for lanes in GROUPS:
            opener_lines[rows, lanes] = of_parent(opener_reach, rows, lanes)

    def free_of(b, begin, size):
        part = slice(begin, begin + size)
        per_card = dot(jnp.concatenate([high[part, :], low[part, :]], 1), counts[...])
        first = per_card.astype(BF16)
        rest = per_card - first.astype(F32)
        second = rest.astype(BF16)
        third = (rest - second.astype(F32)).astype(BF16)
        lane = lax.broadcasted_iota(jnp.int32, (size, 128), 1)
        left = jnp.where(lane < 64, first.astype(F32), second.astype(F32)).astype(BF16)
        free[b, 0:size, :] = dot(jnp.concatenate([left, third], 1), spreads[...])

    def sign_rows(b, rows):
        for lanes in (*GROUPS[:2], slice(1024, HP)):
            gap = rank_rows[b : b + 1, lanes] - wide(rank_columns[b, rows, :], lanes)
            sign = jnp.clip(gap, -1.0, 1.0).astype(BF16)
            signs[b, rows, lanes] = sign * clear[rows, lanes]

    def show(b, begin, size, beside=None):
        part = slice(begin, begin + size)
        for i, at in enumerate(range(0, HP, 256)):
            out = slice(at, min(at + 256, HP))
            shown[b, 0:size, out] = dot(high[part, :], signs[b, :, out])
            if beside is not None:
                beside(i)

    def sign_beside(b, step):
        count = HP // STEP

        @pl.loop(step * count // STEPS, (step + 1) * count // STEPS, unroll=True)
        def _(at):
            sign_rows(b, rows_of(at))

    def opener_ranges(b):
        for copy in loads[b]:
            copy.wait()

        @pl.loop(0, L // STEP, unroll=True)
        def _(step):
            rows = rows_of(step)
            for lanes in GROUPS:
                r0, r1 = regrets[b, 0, rows, lanes], regrets[b, 1, rows, lanes]
                inv = 1.0 / (r0 + r1)
                inverse[b, rows, lanes] = inv
                base = opener_lines[rows, lanes] * living[b, :, lanes] * inv
                for k, r in enumerate((r0, r1)):
                    top, rest = split(base * r)
                    high[rows_of(step, k * L), lanes] = top
                    low[rows_of(step, k * L), lanes] = rest

    def line_copy(step):
        rows = rows_of(step)
        return pltpu.make_async_copy(
            responder_total.at[rows], lines.at[rows, 0, :], line_sems.at[step]
        )

    def responder_values(b, step):
        rows = rows_of(step)
        for lanes in GROUPS:
            base = opener_lines[rows, lanes] * living[b, :, lanes] * inverse[b, rows, lanes]
            value = jnp.zeros(base.shape, F32)
            for k in range(2):
                line = rows_of(step, k * L)
                clean = free[b, line, lanes] + base * regrets[b, k, rows, lanes]
                value = value + wide(columns[1 + k, rows, :], lanes) * shown[b, line, lanes]
                value = value + wide(columns[3 + k, rows, :], lanes) * clean
            value = value * living[b, :, lanes]
            if b == 0:
                responder_total[rows, lanes] = value
            else:
                responder_total[rows, lanes] += value
        if b == 1:
            line_copy(step).start()

    for i in range(PIECES):
        clear_loads[i].wait()

        @pl.loop(i * (HP // STEP) // PIECES, (i + 1) * (HP // STEP) // PIECES, unroll=True)
        def _(step):
            sign_rows(0, rows_of(step))

    gather_stage(1)
    opener_ranges(0)
    show(0, 0, 2 * L, functools.partial(sign_beside, 1))
    gather_stage(2)
    for copy in smalls[-2:]:
        copy.wait()
    free_of(0, 0, 2 * L)
    opener_ranges(1)
    gather_stage(3)
    show(1, 0, 2 * L, functools.partial(responder_values, 0))
    free_of(1, 0, 2 * L)
    for step in range(STEPS):
        responder_values(1, step)

    nexts = [
        [
            remote(
                block_of(lines, me + sign * (7 - 2 * stage)),
                next_slots.at[way, stage],
                next_send.at[way, stage],
                next_recv.at[way, stage],
                along(sign),
            )
            for stage in range(STAGES)
        ]
        for way, sign in enumerate((1, -1))
    ]
    sums = [
        [
            remote(
                sum_out.at[way, stage - 1] if stage else block_of(lines, me + 8),
                sum_slots.at[way, stage],
                sum_send.at[way, stage],
                sum_recv.at[way, stage],
                along(2 * sign),
            )
            if stage or sign > 0
            else None
            for stage in range(STAGES)
        ]
        for way, sign in enumerate((1, -1))
    ]

    def reduce_stage(stage):
        for way, sign in enumerate((1, -1)):
            if stage:
                total = block_of(lines, me + sign * (8 - 2 * stage))[...]
                nexts[way][stage - 1].wait_recv()
                total = total + next_slots[way, stage - 1]
                if stage > 1 or sign > 0:
                    sums[way][stage - 1].wait_recv()
                    total = total + sum_slots[way, stage - 1]
                sum_out[way, stage - 1] = total
            if stage or sign > 0:
                sums[way][stage].start()
            nexts[way][stage].start()

    gather_end()
    turn_load = pltpu.make_async_copy(gathered.at[:, 0, :], turn_lines, turn_sem)
    turn_load.start()
    for step in range(STEPS):
        line_copy(step).wait()
    reduce_stage(0)

    turn_load.wait()

    @pl.loop(0, L // STEP, unroll=True)
    def _(step):
        rows = rows_of(step)
        for lanes in GROUPS:
            top, rest = split(turn_lines[rows, lanes])
            high[rows, lanes] = top
            low[rows, lanes] = rest

    same = (columns[0, :, 0:L] == parents).astype(F32).astype(BF16)
    shown[0, 0:L, :] = dot(same, high[0:L, :]) + dot(same, low[0:L, :])

    @pl.loop(0, L // STEP, unroll=True)
    def _(step):
        rows = rows_of(step)
        for lanes in GROUPS:
            share = turn_lines[rows, lanes] / shown[0, rows, lanes]
            strategy[rows, lanes] = share
            responder_lines[rows, lanes] = of_parent(responder_reach, rows, lanes) * share

    places = (2 * L, 0)

    def responder_ranges(b, step):
        rows = rows_of(step)
        line = rows_of(step, places[b])
        for lanes in GROUPS:
            top, rest = split(responder_lines[rows, lanes] * living[b, :, lanes])
            high[line, lanes] = top
            low[line, lanes] = rest

    def opener_values(b, step):
        rows = rows_of(step)
        for lanes in GROUPS:
            live = living[b, :, lanes]
            inv = inverse[b, rows, lanes]
            won = shown[b, rows, lanes] * live
            lost = (free[b, rows, lanes] + responder_lines[rows, lanes]) * live
            old, values = [], []
            node = jnp.zeros(live.shape, F32)
            for k in range(2):
                old.append(regrets[b, k, rows, lanes])
                values.append(
                    wide(columns[1 + k, rows, :], lanes) * won
                    - wide(columns[3 + k, rows, :], lanes) * lost
                )
                node = node + old[k] * inv * values[k]
            for k in range(2):
                regrets[b, k, rows, lanes] = jnp.maximum(old[k] + values[k] - node, 0.0)
            if b == 0:
                opener_total[rows, lanes] = node
            else:
                top, rest = split(opener_total[rows, lanes] + node)
                high[rows_of(step, 2 * L), lanes] = top
                low[rows_of(step, 2 * L), lanes] = rest

    def beside_first(step):
        responder_ranges(1, step)
        rows = rows_of(step)
        for lanes in GROUPS:
            top, rest = split(responder_total[rows, lanes] * strategy[rows, lanes])
            high[rows_of(step, L), lanes] = top
            low[rows_of(step, L), lanes] = rest

    def store(b):
        copies = [
            pltpu.make_async_copy(
                regrets.at[b, k], new_river.at[0, b, :, k, :], out_sems.at[b, k]
            )
            for k in range(2)
        ]
        start(copies)
        return copies

    for step in range(STEPS):
        responder_ranges(0, step)
    show(0, 2 * L, L, beside_first)
    free_of(0, 2 * L, L)
    show(1, 0, L, functools.partial(opener_values, 0))
    stores = store(0)
    reduce_stage(1)
    free_of(1, 0, L)
    for step in range(STEPS):
        opener_values(1, step)

    flops = lax.broadcasted_iota(jnp.int32, (8, L), 0).astype(F32)
    for_opener = (flops == parents).astype(F32).astype(BF16)
    for_responder = (flops - F == parents).astype(F32).astype(BF16)
    nodes = (
        dot(for_opener, high[2 * L :, :])
        + dot(for_opener, low[2 * L :, :])
        + dot(for_responder, high[L : 2 * L, :])
        + dot(for_responder, low[L : 2 * L, :])
    )
    for i in range(8):
        parts[i] = nodes[i : i + 1, 0:HALF]
        parts[8 + i, :, 0 : HP - HALF] = nodes[i : i + 1, HALF:HP]
        parts[8 + i, :, HP - HALF :] = jnp.zeros((1, 2 * HALF - HP), F32)

    def exchange(src_of, slots, semaphores, offsets, peers):
        send, recv = semaphores
        copies = [
            remote(src_of(peer), slots.at[d], send, recv, peer)
            for d, peer in zip(offsets, peers)
        ]
        start(copies)

    def landed(slots, semaphores):
        pltpu.make_async_copy(
            slots.at[pl.ds(1, slots.shape[0] - 1)],
            slots.at[pl.ds(1, slots.shape[0] - 1)],
            semaphores[1],
        ).wait()

    def sent(slots, semaphores):
        pltpu.make_async_copy(
            slots.at[pl.ds(1, slots.shape[0] - 1)],
            slots.at[pl.ds(1, slots.shape[0] - 1)],
            semaphores[0],
        ).wait()

    def sum_of(slots):
        total = slots[0]
        for d in range(1, slots.shape[0]):
            total = total + slots[d]
        return total

    part_sems = (part_send, part_recv)
    plane_sems = (plane_send, plane_recv)
    row_sems = (row_send, row_recv)
    node_sems = (node_send, node_recv)
    final_sems = (final_send, final_recv)
    exchange(lambda peer: parts.at[peer[1]], part_slots, part_sems, distances, line_peers)
    part_slots[0] = parts[me]
    reduce_stage(2)
    landed(part_slots, part_sems)
    total = sum_of(part_slots)
    plane_slots[0] = total
    all_nodes[0] = total
    exchange(lambda peer: plane_slots.at[0], plane_slots, plane_sems, range(1, 8), plane_peers)
    reduce_stage(3)
    for copy in (
        sum((stage for way in gathers for half in way for stage in half), []) + nexts[0][:3] + nexts[1][:3]
    ):
        copy.wait_send()

    landed(plane_slots, plane_sems)
    row_slots[0] = sum_of(plane_slots)
    exchange(lambda peer: row_slots.at[0], row_slots, row_sems, range(1, 4), row_peers)
    exchange(lambda peer: all_nodes.at[0], all_nodes, node_sems, distances, line_peers)
    landed(row_slots, row_sems)
    finals[0] = sum_of(row_slots) * (1.0 / (32 * 32))
    exchange(lambda peer: finals.at[0], finals, final_sems, distances, line_peers)
    stores = stores + store(1)

    def chunk(slots, at):
        return slots[lax.rem(me - at + Z, Z)]

    landed(all_nodes, node_sems)
    total = block_of(lines, me)[...]
    for way in range(2):
        nexts[way][-1].wait_recv()
        sums[way][-1].wait_recv()
        total = total + next_slots[way, STAGES - 1] + sum_slots[way, STAGES - 1]
    own = block_of(gathered, me)
    lane = lax.broadcasted_iota(jnp.int32, (1, L), 1)
    for i in range(OWN):
        mine = jnp.sum(
            jnp.where(lane == me * OWN + i, parents, 0.0), axis=1, keepdims=True
        )
        node_low, node_high = chunk(all_nodes, F), chunk(all_nodes, 8 + F)
        for f in range(1, F):
            node_low = jnp.where(mine == f, chunk(all_nodes, F + f), node_low)
            node_high = jnp.where(mine == f, chunk(all_nodes, 8 + F + f), node_high)
        new_turn[i, :, 0:HALF] = jnp.maximum(
            own[i, :, 0:HALF] + (total[i, :, 0:HALF] - node_low) * (1.0 / 32), 0.0
        )
        new_turn[i, :, HALF:H] = jnp.maximum(
            own[i, :, HALF:H]
            + (total[i, :, HALF:H] - node_high[:, 0 : H - HALF]) * (1.0 / 32),
            0.0,
        )

    landed(finals, final_sems)
    for i in range(8):
        player, f = i // F, i % F
        flop[player, f : f + 1, 0:HALF] = chunk(finals, i)
        flop[player, f : f + 1, HALF:H] = chunk(finals, 8 + i)[:, 0 : H - HALF]
    for copy in stores:
        copy.wait()
    for copy in nexts[0][3:] + nexts[1][3:] + sums[0] + sums[1][1:]:
        copy.wait_send()
    sent(part_slots, part_sems)
    sent(plane_slots, plane_sems)
    sent(row_slots, row_sems)
    sent(all_nodes, node_sems)
    sent(finals, final_sems)


def iterate(
    opener_reach,
    responder_reach,
    turn_parent,
    turn_cards,
    river_cards,
    showdown_ranks,
    fold_mask,
    half_pot,
    own,
    river_regrets,
):
    clear, counts, spreads, cards = tables()
    vmem = pl.BlockSpec(memory_space=pltpu.VMEM)
    hbm = pl.BlockSpec(memory_space=pltpu.HBM)
    dma = pltpu.SemaphoreType.DMA
    return pl.pallas_call(
        kernel,
        out_shape=(
            jax.ShapeDtypeStruct((OWN, 1, H), F32),
            jax.ShapeDtypeStruct(river_regrets.shape, F32),
            jax.ShapeDtypeStruct((2, F, H), F32),
        ),
        in_specs=[hbm] * 14,
        out_specs=(vmem, vmem, vmem),
        scratch_shapes=[
            pltpu.VMEM((F, H), F32),
            pltpu.VMEM((F, H), F32),
            pltpu.VMEM((1, L), jnp.int32),
            pltpu.VMEM((1, 1), jnp.int32),
            pltpu.VMEM((1, BOARDS), jnp.int32),
            pltpu.VMEM((1, BOARDS, H), jnp.int32),
            pltpu.VMEM((2, L), jnp.int32),
            pltpu.VMEM((2, L), F32),
            pltpu.VMEM((2 * HP, 128), BF16),
            pltpu.VMEM((256, HP), BF16),
            pltpu.VMEM((8, HP), jnp.int32),
            pltpu.VMEM((HP, HP), BF16),
            pltpu.VMEM((BOARDS, 2, L, H), F32),
            pltpu.VMEM((L, 1, H), F32),
            pltpu.VMEM((L, H), F32),
            pltpu.VMEM((BOARDS, HP, HP), BF16),
            pltpu.VMEM((BOARDS, L, H), F32),
            pltpu.VMEM((L, H), F32),
            pltpu.VMEM((L, H), F32),
            pltpu.VMEM((L, H), F32),
            pltpu.VMEM((3 * L, HP), BF16),
            pltpu.VMEM((3 * L, HP), BF16),
            pltpu.VMEM((BOARDS, 2 * L, HP), F32),
            pltpu.VMEM((BOARDS, 2 * L, HP), F32),
            pltpu.VMEM((5, L, 128), F32),
            pltpu.VMEM((BOARDS, STEP, HP), F32),
            pltpu.VMEM((8, HP), F32),
            pltpu.VMEM((BOARDS, HP, 128), F32),
            pltpu.VMEM((L, HP), F32),
            pltpu.VMEM((L, HP), F32),
            pltpu.VMEM((L, 1, HP), F32),
            pltpu.VMEM((Z, 1, HALF), F32),
            pltpu.VMEM((Z, 1, HALF), F32),
            pltpu.VMEM((Z, 1, HALF), F32),
            pltpu.VMEM((8, 1, HALF), F32),
            pltpu.VMEM((4, 1, HALF), F32),
            pltpu.VMEM((Z, 1, HALF), F32),
            pltpu.VMEM((2, STAGES, OWN, 1, HP), F32),
            pltpu.VMEM((2, STAGES, OWN, 1, HP), F32),
            pltpu.VMEM((2, STAGES - 1, OWN, 1, HP), F32),
            dma((11,)),
            dma((PIECES,)),
            dma,
            dma((BOARDS, 2)),
            dma,
            dma((L // STEP,)),
            dma((BOARDS, 2)),
        ]
        + [
            dma(shape)
            for shape in ((2, 2, STAGES, 2), (2, STAGES), (2, STAGES))
            for _ in range(2)
        ]
        + [dma] * 10,
        compiler_params=pltpu.CompilerParams(
            collective_id=0, has_side_effects=True, vmem_limit_bytes=46 * MIB
        ),
    )(
        *(
            pltpu.with_memory_space_constraint(operand, pltpu.HBM) if operand.size > 1 else operand
            for operand in (
                opener_reach,
                responder_reach,
                turn_parent.reshape(1, L),
                turn_cards.reshape(1, 1),
                river_cards,
                showdown_ranks,
                fold_mask.T,
                half_pot.T,
                jnp.asarray(counts),
                jnp.asarray(spreads),
                jnp.asarray(cards),
                jnp.asarray(clear),
                own,
                river_regrets,
            )
        )
    )


def on_device(
    opener_reach,
    responder_reach,
    turn_parent,
    turn_cards,
    river_cards,
    showdown_ranks,
    fold_mask,
    half_pot,
    turn_regrets,
    river_regrets,
):
    new_turn, new_river, flop_values = iterate(
        opener_reach,
        responder_reach,
        turn_parent,
        turn_cards,
        river_cards,
        showdown_ranks,
        fold_mask,
        half_pot,
        turn_regrets.reshape(OWN, 1, H),
        river_regrets,
    )
    return new_turn.reshape(1, OWN, H), new_river, flop_values


def solution(mesh):
    placed = (
        P(),
        P(),
        P(),
        P("turn"),
        P("turn", "river"),
        P("turn", "river", None),
        P(),
        P(),
        P("turn", "river", None),
        P("turn", "river", None, None, None),
    )
    return jax.shard_map(
        on_device,
        mesh=mesh,
        in_specs=placed,
        out_specs=(P("turn", "river", None), P("turn", "river", None, None, None), P()),
        check_vma=False,
    )
```

```python
import functools

import jax
import jax.numpy as jnp
import numpy as np
from jax import lax
from jax.experimental import pallas as pl
from jax.experimental.pallas import tpu as pltpu
from jax.sharding import PartitionSpec as P

MESH = pl.DeviceIdType.MESH
F32 = jnp.float32
BF16 = jnp.bfloat16

H = 1326
HP = 1408
L = 96
F = 4
Z = 16
OWN = L // Z
BOARDS = 2
HALF = 768
STEP = 16
STEPS = L // STEP
STAGES = Z // 4
MIB = 2**20
GROUPS = (slice(0, 512), slice(512, 1024), slice(1024, H))


def tables():
    low, high = np.triu_indices(52, 1)
    holds = np.zeros((HP, 64), np.float32)
    holds[np.arange(H), low] = 1.0
    holds[np.arange(H), high] = 1.0
    clear = (holds @ holds.T == 0).astype(np.float32)
    clear[H:] = 0.0
    clear[:, H:] = 0.0
    counts = holds.copy()
    counts[:H, 52] = 1.0
    spread = -holds.T.copy()
    spread[52, :H] = 1.0
    spreads = np.concatenate([spread, spread, spread, np.zeros_like(spread)], 0)
    cards = np.full((8, HP), -1, np.int32)
    cards[0, :H] = low
    cards[1, :H] = high
    return (
        clear.astype(BF16),
        np.tile(counts, (2, 2)).astype(BF16),
        spreads.astype(BF16),
        cards,
    )


def split(value):
    high = value.astype(BF16)
    return high, (value - high.astype(F32)).astype(BF16)


def dot(a, b):
    return jnp.dot(a, b, preferred_element_type=F32)


def column(row):
    return jnp.broadcast_to(row, (128, row.shape[1])).T


def wide(tile, lanes):
    width = lanes.stop - lanes.start
    return jnp.concatenate([tile] * (-(-width // 128)), 1)[:, :width]


def rows_of(step, start=0):
    if isinstance(step, int):
        return slice(step * STEP + start, step * STEP + start + STEP)
    return pl.ds(pl.multiple_of(step * STEP + start, STEP), STEP)


def kernel(
    opener_hbm,
    responder_hbm,
    parent_hbm,
    turn_card_hbm,
    river_cards_hbm,
    ranks_hbm,
    fold_hbm,
    pot_hbm,
    counts_hbm,
    spreads_hbm,
    cards_hbm,
    clear_hbm,
    own_hbm,
    river_hbm,
    new_turn,
    new_river,
    flop,
    opener_reach,
    responder_reach,
    parent_row,
    turn_card,
    river_cards,
    ranks,
    fold,
    pot,
    counts,
    spreads,
    cards,
    clear,
    pairs,
    regrets,
    gathered,
    turn_lines,
    signs,
    inverse,
    opener_lines,
    strategy,
    responder_lines,
    high,
    low,
    shown,
    free,
    columns,
    living,
    rank_rows,
    rank_columns,
    opener_total,
    responder_total,
    lines,
    parts,
    part_slots,
    all_nodes,
    plane_slots,
    row_slots,
    finals,
    next_slots,
    sum_slots,
    sum_out,
    small_sems,
    clear_sem,
    own_sem,
    in_sems,
    turn_sem,
    line_sems,
    gather_send,
    gather_recv,
    next_send,
    next_recv,
    sum_send,
    sum_recv,
    part_send,
    part_recv,
    node_send,
    node_recv,
    plane_send,
    plane_recv,
    row_send,
    row_recv,
    final_send,
    final_recv,
):
    me = lax.axis_index("river")
    turn = lax.axis_index("turn")
    row, place = turn // 8, lax.rem(turn, 8)

    def along(distance):
        return (turn, lax.rem(me + distance + Z, Z))

    distances = sorted(range(1, Z), key=lambda d: -min(d, Z - d))
    line_peers = [along(d) for d in distances]
    plane_peers = [(row * 8 + lax.rem(place + d, 8), me) for d in range(1, 8)]
    row_peers = [(lax.rem(row + d, 4) * 8 + place, me) for d in range(1, 4)]
    everyone = line_peers + plane_peers + row_peers
    barrier = pltpu.get_barrier_semaphore()
    for peer in everyone:
        pl.semaphore_signal(barrier, inc=1, device_id=peer, device_id_type=MESH)

    def block_of(ref, owner):
        return ref.at[pl.ds(lax.rem(owner + Z, Z) * OWN, OWN)]

    def remote(src, dst, send, recv, peer):
        return pltpu.make_async_remote_copy(
            src_ref=src,
            dst_ref=dst,
            send_sem=send,
            recv_sem=recv,
            device_id=peer,
            device_id_type=MESH,
        )

    def start(copies):
        for copy in copies:
            copy.start()

    def arrive(copies):
        for copy in copies:
            copy.wait_recv()

    own_load = pltpu.make_async_copy(own_hbm, block_of(gathered, me), own_sem)
    own_load.start()
    smalls = [
        pltpu.make_async_copy(src, dst, small_sems.at[i])
        for i, (src, dst) in enumerate(
            (
                (opener_hbm, opener_reach),
                (responder_hbm, responder_reach),
                (parent_hbm, parent_row),
                (turn_card_hbm, turn_card),
                (river_cards_hbm, river_cards),
                (ranks_hbm, ranks),
                (fold_hbm, fold),
                (pot_hbm, pot),
                (cards_hbm, cards),
                (counts_hbm, counts),
                (spreads_hbm, spreads),
            )
        )
    ]
    start(smalls)
    loads = [
        pltpu.make_async_copy(river_hbm.at[0, b], pairs.at[b], in_sems.at[b])
        for b in range(BOARDS)
    ]
    clear_load = pltpu.make_async_copy(clear_hbm, clear, clear_sem)
    loads[0].start()
    clear_load.start()
    loads[1].start()
    gathers = [
        [
            [
                remote(
                    block_of(gathered, me - sign * 2 * stage) if stage else own_hbm,
                    block_of(gathered, me - sign * 2 * stage),
                    gather_send.at[way, stage, far],
                    gather_recv.at[way, stage, far],
                    along(sign * (1 + far)),
                )
                for far in range(1 if sign < 0 and stage == STAGES - 1 else 2)
            ]
            for stage in range(STAGES)
        ]
        for way, sign in enumerate((1, -1))
    ]

    def gather_stage(stage):
        for way in gathers:
            if stage:
                way[stage - 1][1].wait_recv()
            start(way[stage][::-1])

    def gather_end():
        for way in gathers:
            for stage in range(STAGES):
                way[stage][0].wait_recv()
        gathers[0][-1][1].wait_recv()

    pl.semaphore_wait(barrier, len(everyone))
    gather_stage(0)
    for copy in [own_load] + smalls:
        copy.wait()

    parents = parent_row[...].astype(F32)
    columns[0] = column(parents)
    for k in range(2):
        folded = fold[k : k + 1, :].astype(F32)
        stake = pot[k : k + 1, :]
        columns[1 + k] = column(stake * (1.0 - folded))
        columns[3 + k] = column(stake * folded)
    for b in range(BOARDS):
        dead = jnp.zeros((1, HP), jnp.bool_)
        for card in (turn_card[...], river_cards[:, b : b + 1]):
            dead = dead | (cards[0:1, :] == card) | (cards[1:2, :] == card)
        living[b] = jnp.broadcast_to(jnp.where(dead, 0.0, 1.0).astype(F32), (STEP, HP))
    rank_rows[:, HP - 128 :] = jnp.zeros((8, 128), F32)
    rank_rows[0:BOARDS, 0:H] = ranks[0].astype(F32)
    high[:, HP - 128 :] = jnp.zeros((3 * L, 128), BF16)
    low[:, HP - 128 :] = jnp.zeros((3 * L, 128), BF16)
    responder_total[:, HP - 128 :] = jnp.zeros((L, 128), F32)
    for b in range(BOARDS):
        for c in range(HP // 128):
            tile = slice(c * 128, c * 128 + 128)
            rank_columns[b, tile, :] = column(rank_rows[b : b + 1, tile])

    def of_parent(reach, rows, lanes):
        parent = wide(columns[0, rows, :], lanes)
        line = jnp.broadcast_to(reach[0:1, lanes], parent.shape)
        for f in range(1, F):
            line = jnp.where(parent == f, reach[f : f + 1, lanes], line)
        return line

    @pl.loop(0, L // STEP, unroll=True)
    def _(step):
        rows = rows_of(step)
        for lanes in GROUPS:
            opener_lines[rows, lanes] = of_parent(opener_reach, rows, lanes)

    def free_of(b, begin, size):
        part = slice(begin, begin + size)
        per_card = dot(jnp.concatenate([high[part, :], low[part, :]], 1), counts[...])
        first = per_card.astype(BF16)
        rest = per_card - first.astype(F32)
        second = rest.astype(BF16)
        third = (rest - second.astype(F32)).astype(BF16)
        lane = lax.broadcasted_iota(jnp.int32, (size, 128), 1)
        left = jnp.where(lane < 64, first.astype(F32), second.astype(F32)).astype(BF16)
        free[b, 0:size, :] = dot(jnp.concatenate([left, third], 1), spreads[...])

    def sign_rows(b, rows):
        for lanes in (*GROUPS[:2], slice(1024, HP)):
            gap = rank_rows[b : b + 1, lanes] - wide(rank_columns[b, rows, :], lanes)
            sign = jnp.clip(gap, -1.0, 1.0).astype(BF16)
            signs[b, rows, lanes] = sign * clear[rows, lanes]

    def show(b, begin, size, beside=None):
        part = slice(begin, begin + size)
        for i, at in enumerate(range(0, HP, 256)):
            out = slice(at, min(at + 256, HP))
            shown[b, 0:size, out] = dot(high[part, :], signs[b, :, out])
            if beside is not None:
                beside(i)

    def sign_beside(b, step):
        count = HP // STEP

        @pl.loop(step * count // STEPS, (step + 1) * count // STEPS, unroll=True)
        def _(at):
            sign_rows(b, rows_of(at))

    def opener_ranges(b):
        loads[b].wait()

        @pl.loop(0, L // STEP, unroll=True)
        def _(step):
            rows = rows_of(step)
            for lanes in GROUPS:
                r0, r1 = pairs[b, rows, 0, lanes], pairs[b, rows, 1, lanes]
                regrets[b, 0, rows, lanes] = r0
                regrets[b, 1, rows, lanes] = r1
                inv = 1.0 / (r0 + r1)
                inverse[b, rows, lanes] = inv
                base = opener_lines[rows, lanes] * living[b, :, lanes] * inv
                for k, r in enumerate((r0, r1)):
                    top, rest = split(base * r)
                    high[rows_of(step, k * L), lanes] = top
                    low[rows_of(step, k * L), lanes] = rest

    def line_copy(step):
        rows = rows_of(step)
        return pltpu.make_async_copy(
            responder_total.at[rows], lines.at[rows, 0, :], line_sems.at[step]
        )

    def responder_values(b, step):
        rows = rows_of(step)
        for lanes in GROUPS:
            base = opener_lines[rows, lanes] * living[b, :, lanes] * inverse[b, rows, lanes]
            value = jnp.zeros(base.shape, F32)
            for k in range(2):
                line = rows_of(step, k * L)
                clean = free[b, line, lanes] + base * regrets[b, k, rows, lanes]
                value = value + wide(columns[1 + k, rows, :], lanes) * shown[b, line, lanes]
                value = value + wide(columns[3 + k, rows, :], lanes) * clean
            value = value * living[b, :, lanes]
            if b == 0:
                responder_total[rows, lanes] = value
            else:
                responder_total[rows, lanes] += value
        if b == 1:
            line_copy(step).start()

    clear_load.wait()

    @pl.loop(0, HP // STEP, unroll=True)
    def _(step):
        sign_rows(0, rows_of(step))

    gather_stage(1)
    opener_ranges(0)
    show(0, 0, 2 * L, functools.partial(sign_beside, 1))
    gather_stage(2)
    free_of(0, 0, 2 * L)
    opener_ranges(1)
    gather_stage(3)
    show(1, 0, 2 * L, functools.partial(responder_values, 0))
    free_of(1, 0, 2 * L)
    for step in range(STEPS):
        responder_values(1, step)

    nexts = [
        [
            remote(
                block_of(lines, me + sign * (7 - 2 * stage)),
                next_slots.at[way, stage],
                next_send.at[way, stage],
                next_recv.at[way, stage],
                along(sign),
            )
            for stage in range(STAGES)
        ]
        for way, sign in enumerate((1, -1))
    ]
    sums = [
        [
            remote(
                sum_out.at[way, stage - 1] if stage else block_of(lines, me + 8),
                sum_slots.at[way, stage],
                sum_send.at[way, stage],
                sum_recv.at[way, stage],
                along(2 * sign),
            )
            if stage or sign > 0
            else None
            for stage in range(STAGES)
        ]
        for way, sign in enumerate((1, -1))
    ]

    def reduce_stage(stage):
        for way, sign in enumerate((1, -1)):
            if stage:
                total = block_of(lines, me + sign * (8 - 2 * stage))[...]
                nexts[way][stage - 1].wait_recv()
                total = total + next_slots[way, stage - 1]
                if stage > 1 or sign > 0:
                    sums[way][stage - 1].wait_recv()
                    total = total + sum_slots[way, stage - 1]
                sum_out[way, stage - 1] = total
            if stage or sign > 0:
                sums[way][stage].start()
            nexts[way][stage].start()

    gather_end()
    turn_load = pltpu.make_async_copy(gathered.at[:, 0, :], turn_lines, turn_sem)
    turn_load.start()
    for step in range(STEPS):
        line_copy(step).wait()
    reduce_stage(0)

    turn_load.wait()

    @pl.loop(0, L // STEP, unroll=True)
    def _(step):
        rows = rows_of(step)
        for lanes in GROUPS:
            top, rest = split(turn_lines[rows, lanes])
            high[rows, lanes] = top
            low[rows, lanes] = rest

    same = (columns[0, :, 0:L] == parents).astype(F32).astype(BF16)
    shown[0, 0:L, :] = dot(same, high[0:L, :]) + dot(same, low[0:L, :])

    @pl.loop(0, L // STEP, unroll=True)
    def _(step):
        rows = rows_of(step)
        for lanes in GROUPS:
            share = turn_lines[rows, lanes] / shown[0, rows, lanes]
            strategy[rows, lanes] = share
            responder_lines[rows, lanes] = of_parent(responder_reach, rows, lanes) * share

    places = (2 * L, 0)

    def responder_ranges(b, step):
        rows = rows_of(step)
        line = rows_of(step, places[b])
        for lanes in GROUPS:
            top, rest = split(responder_lines[rows, lanes] * living[b, :, lanes])
            high[line, lanes] = top
            low[line, lanes] = rest

    def opener_values(b, step):
        rows = rows_of(step)
        for lanes in GROUPS:
            live = living[b, :, lanes]
            inv = inverse[b, rows, lanes]
            won = shown[b, rows, lanes] * live
            lost = (free[b, rows, lanes] + responder_lines[rows, lanes]) * live
            old, values = [], []
            node = jnp.zeros(live.shape, F32)
            for k in range(2):
                old.append(regrets[b, k, rows, lanes])
                values.append(
                    wide(columns[1 + k, rows, :], lanes) * won
                    - wide(columns[3 + k, rows, :], lanes) * lost
                )
                node = node + old[k] * inv * values[k]
            for k in range(2):
                new_river[0, b, rows, k, lanes] = jnp.maximum(old[k] + values[k] - node, 0.0)
            if b == 0:
                opener_total[rows, lanes] = node
            else:
                top, rest = split(opener_total[rows, lanes] + node)
                high[rows_of(step, 2 * L), lanes] = top
                low[rows_of(step, 2 * L), lanes] = rest

    def beside_first(step):
        responder_ranges(1, step)
        rows = rows_of(step)
        for lanes in GROUPS:
            top, rest = split(responder_total[rows, lanes] * strategy[rows, lanes])
            high[rows_of(step, L), lanes] = top
            low[rows_of(step, L), lanes] = rest

    for step in range(STEPS):
        responder_ranges(0, step)
    show(0, 2 * L, L, beside_first)
    free_of(0, 2 * L, L)
    reduce_stage(1)
    show(1, 0, L, functools.partial(opener_values, 0))
    free_of(1, 0, L)
    for step in range(STEPS):
        opener_values(1, step)

    flops = lax.broadcasted_iota(jnp.int32, (8, L), 0).astype(F32)
    for_opener = (flops == parents).astype(F32).astype(BF16)
    for_responder = (flops - F == parents).astype(F32).astype(BF16)
    nodes = (
        dot(for_opener, high[2 * L :, :])
        + dot(for_opener, low[2 * L :, :])
        + dot(for_responder, high[L : 2 * L, :])
        + dot(for_responder, low[L : 2 * L, :])
    )
    for i in range(8):
        parts[i] = nodes[i : i + 1, 0:HALF]
        parts[8 + i, :, 0 : HP - HALF] = nodes[i : i + 1, HALF:HP]
        parts[8 + i, :, HP - HALF :] = jnp.zeros((1, 2 * HALF - HP), F32)

    def exchange(src_of, slots, semaphores, offsets, peers):
        send, recv = semaphores
        copies = [
            remote(src_of(peer), slots.at[d], send, recv, peer)
            for d, peer in zip(offsets, peers)
        ]
        start(copies)

    def landed(slots, semaphores):
        pltpu.make_async_copy(
            slots.at[pl.ds(1, slots.shape[0] - 1)],
            slots.at[pl.ds(1, slots.shape[0] - 1)],
            semaphores[1],
        ).wait()

    def sent(slots, semaphores):
        pltpu.make_async_copy(
            slots.at[pl.ds(1, slots.shape[0] - 1)],
            slots.at[pl.ds(1, slots.shape[0] - 1)],
            semaphores[0],
        ).wait()

    def sum_of(slots):
        total = slots[0]
        for d in range(1, slots.shape[0]):
            total = total + slots[d]
        return total

    part_sems = (part_send, part_recv)
    plane_sems = (plane_send, plane_recv)
    row_sems = (row_send, row_recv)
    node_sems = (node_send, node_recv)
    final_sems = (final_send, final_recv)
    exchange(lambda peer: parts.at[peer[1]], part_slots, part_sems, distances, line_peers)
    part_slots[0] = parts[me]
    reduce_stage(2)
    landed(part_slots, part_sems)
    total = sum_of(part_slots)
    plane_slots[0] = total
    all_nodes[0] = total
    exchange(lambda peer: plane_slots.at[0], plane_slots, plane_sems, range(1, 8), plane_peers)
    reduce_stage(3)
    for copy in (
        sum((stage for way in gathers for stage in way), []) + nexts[0][:3] + nexts[1][:3]
    ):
        copy.wait_send()

    landed(plane_slots, plane_sems)
    row_slots[0] = sum_of(plane_slots)
    exchange(lambda peer: row_slots.at[0], row_slots, row_sems, range(1, 4), row_peers)
    exchange(lambda peer: all_nodes.at[0], all_nodes, node_sems, distances, line_peers)
    landed(row_slots, row_sems)
    finals[0] = sum_of(row_slots) * (1.0 / (32 * 32))
    exchange(lambda peer: finals.at[0], finals, final_sems, distances, line_peers)

    def chunk(slots, at):
        return slots[lax.rem(me - at + Z, Z)]

    landed(all_nodes, node_sems)
    total = block_of(lines, me)[...]
    for way in range(2):
        nexts[way][-1].wait_recv()
        sums[way][-1].wait_recv()
        total = total + next_slots[way, STAGES - 1] + sum_slots[way, STAGES - 1]
    own = block_of(gathered, me)
    lane = lax.broadcasted_iota(jnp.int32, (1, L), 1)
    for i in range(OWN):
        mine = jnp.sum(
            jnp.where(lane == me * OWN + i, parents, 0.0), axis=1, keepdims=True
        )
        node_low, node_high = chunk(all_nodes, F), chunk(all_nodes, 8 + F)
        for f in range(1, F):
            node_low = jnp.where(mine == f, chunk(all_nodes, F + f), node_low)
            node_high = jnp.where(mine == f, chunk(all_nodes, 8 + F + f), node_high)
        new_turn[i, :, 0:HALF] = jnp.maximum(
            own[i, :, 0:HALF] + (total[i, :, 0:HALF] - node_low) * (1.0 / 32), 0.0
        )
        new_turn[i, :, HALF:H] = jnp.maximum(
            own[i, :, HALF:H]
            + (total[i, :, HALF:H] - node_high[:, 0 : H - HALF]) * (1.0 / 32),
            0.0,
        )

    landed(finals, final_sems)
    for i in range(8):
        player, f = i // F, i % F
        flop[player, f : f + 1, 0:HALF] = chunk(finals, i)
        flop[player, f : f + 1, HALF:H] = chunk(finals, 8 + i)[:, 0 : H - HALF]
    for copy in nexts[0][3:] + nexts[1][3:] + sums[0] + sums[1][1:]:
        copy.wait_send()
    sent(part_slots, part_sems)
    sent(plane_slots, plane_sems)
    sent(row_slots, row_sems)
    sent(all_nodes, node_sems)
    sent(finals, final_sems)


def iterate(
    opener_reach,
    responder_reach,
    turn_parent,
    turn_cards,
    river_cards,
    showdown_ranks,
    fold_mask,
    half_pot,
    own,
    river_regrets,
):
    clear, counts, spreads, cards = tables()
    vmem = pl.BlockSpec(memory_space=pltpu.VMEM)
    hbm = pl.BlockSpec(memory_space=pltpu.HBM)
    dma = pltpu.SemaphoreType.DMA
    return pl.pallas_call(
        kernel,
        out_shape=(
            jax.ShapeDtypeStruct((OWN, 1, H), F32),
            jax.ShapeDtypeStruct(river_regrets.shape, F32),
            jax.ShapeDtypeStruct((2, F, H), F32),
        ),
        in_specs=[hbm] * 14,
        out_specs=(vmem, vmem, vmem),
        scratch_shapes=[
            pltpu.VMEM((F, H), F32),
            pltpu.VMEM((F, H), F32),
            pltpu.VMEM((1, L), jnp.int32),
            pltpu.VMEM((1, 1), jnp.int32),
            pltpu.VMEM((1, BOARDS), jnp.int32),
            pltpu.VMEM((1, BOARDS, H), jnp.int32),
            pltpu.VMEM((2, L), jnp.int32),
            pltpu.VMEM((2, L), F32),
            pltpu.VMEM((2 * HP, 128), BF16),
            pltpu.VMEM((256, HP), BF16),
            pltpu.VMEM((8, HP), jnp.int32),
            pltpu.VMEM((HP, HP), BF16),
            pltpu.VMEM((BOARDS, L, 2, H), F32),
            pltpu.VMEM((BOARDS, 2, L, H), F32),
            pltpu.VMEM((L, 1, H), F32),
            pltpu.VMEM((L, H), F32),
            pltpu.VMEM((BOARDS, HP, HP), BF16),
            pltpu.VMEM((BOARDS, L, H), F32),
            pltpu.VMEM((L, H), F32),
            pltpu.VMEM((L, H), F32),
            pltpu.VMEM((L, H), F32),
            pltpu.VMEM((3 * L, HP), BF16),
            pltpu.VMEM((3 * L, HP), BF16),
            pltpu.VMEM((BOARDS, 2 * L, HP), F32),
            pltpu.VMEM((BOARDS, 2 * L, HP), F32),
            pltpu.VMEM((5, L, 128), F32),
            pltpu.VMEM((BOARDS, STEP, HP), F32),
            pltpu.VMEM((8, HP), F32),
            pltpu.VMEM((BOARDS, HP, 128), F32),
            pltpu.VMEM((L, HP), F32),
            pltpu.VMEM((L, HP), F32),
            pltpu.VMEM((L, 1, HP), F32),
            pltpu.VMEM((Z, 1, HALF), F32),
            pltpu.VMEM((Z, 1, HALF), F32),
            pltpu.VMEM((Z, 1, HALF), F32),
            pltpu.VMEM((8, 1, HALF), F32),
            pltpu.VMEM((4, 1, HALF), F32),
            pltpu.VMEM((Z, 1, HALF), F32),
            pltpu.VMEM((2, STAGES, OWN, 1, HP), F32),
            pltpu.VMEM((2, STAGES, OWN, 1, HP), F32),
            pltpu.VMEM((2, STAGES - 1, OWN, 1, HP), F32),
            dma((11,)),
            dma,
            dma,
            dma((BOARDS,)),
            dma,
            dma((L // STEP,)),
        ]
        + [
            dma(shape)
            for shape in ((2, STAGES, 2), (2, STAGES), (2, STAGES))
            for _ in range(2)
        ]
        + [dma] * 10,
        compiler_params=pltpu.CompilerParams(
            collective_id=0, has_side_effects=True, vmem_limit_bytes=46 * MIB
        ),
    )(
        *(
            pltpu.with_memory_space_constraint(operand, pltpu.HBM) if operand.size > 1 else operand
            for operand in (
                opener_reach,
                responder_reach,
                turn_parent.reshape(1, L),
                turn_cards.reshape(1, 1),
                river_cards,
                showdown_ranks,
                fold_mask.T,
                half_pot.T,
                jnp.asarray(counts),
                jnp.asarray(spreads),
                jnp.asarray(cards),
                jnp.asarray(clear),
                own,
                river_regrets,
            )
        )
    )


def on_device(
    opener_reach,
    responder_reach,
    turn_parent,
    turn_cards,
    river_cards,
    showdown_ranks,
    fold_mask,
    half_pot,
    turn_regrets,
    river_regrets,
):
    new_turn, new_river, flop_values = iterate(
        opener_reach,
        responder_reach,
        turn_parent,
        turn_cards,
        river_cards,
        showdown_ranks,
        fold_mask,
        half_pot,
        turn_regrets.reshape(OWN, 1, H),
        river_regrets,
    )
    return new_turn.reshape(1, OWN, H), new_river, flop_values


def solution(mesh):
    placed = (
        P(),
        P(),
        P(),
        P("turn"),
        P("turn", "river"),
        P("turn", "river", None),
        P(),
        P(),
        P("turn", "river", None),
        P("turn", "river", None, None, None),
    )
    return jax.shard_map(
        on_device,
        mesh=mesh,
        in_specs=placed,
        out_specs=(P("turn", "river", None), P("turn", "river", None, None, None), P()),
        check_vma=False,
    )
```
